128 devices in a mesh: dp: 4 (over z_lo, core), list: 32 (over z_hi, x, y).
Axes of the slice: x: 4, y: 4, z: 4 (z_hi: 2, z_lo: 2; z = z_hi * 2 + z_lo), core: 2. Of those that a mesh axis runs over, the one named last changes fastest.
Arguments:
- passages: bfloat16 [65536, 768], P(('dp', 'list')), may hold values from -8 to 8
- centroids: bfloat16 [8192, 768], P('list'), may hold values from -6 to 6
Outputs:
- new_centroids: float32 [8192, 768], P('list', 'dp')
- list_mass: float32 [8192], P('list')
The draws below stay inside these ranges and needn't reach their ends.
All inputs are finite; a program needn't handle non-finite values.
Results may differ from the reference program's by a relative error of at most 0.0065.
Values may be sent and summed in bfloat16 or wider, within the bound.
A program may use at most 128 MiB of HBM per device.

```python
import jax
import jax.numpy as jnp
from jax import lax

D = 768
K = 8192
ITERS = 3
ROWS = 65536


def shared_centres(key):
    return jnp.clip(jax.random.normal(key, (K, D), jnp.float32), -4.0, 4.0)


def draw_centroids(key, part):
    base = shared_centres(key)
    key = jax.random.fold_in(key, 11)
    jitter = 0.5 * jax.random.normal(key, (K, D), jnp.float32)
    return jnp.clip(base + jitter, -6.0, 6.0).astype(jnp.bfloat16)


def draw_passages(key, part):
    base = shared_centres(key)
    key = jax.random.fold_in(key, 23)
    key_order = jax.random.fold_in(key, 1)
    key_mix = jax.random.fold_in(key, 5)
    key_noise = jax.random.fold_in(key, 6)
    order = jax.random.permutation(key_order, K).astype(jnp.int32)
    lowest = jax.random.randint(jax.random.fold_in(key, 40), (ROWS,), 0, K, jnp.int32)
    for draw_number in range(5):
        other = jax.random.randint(jax.random.fold_in(key, 41 + draw_number), (ROWS,), 0, K, jnp.int32)
        lowest = jnp.minimum(lowest, other)
    owner = order[lowest]
    mixing = jax.random.uniform(key_mix, (ROWS, 1), jnp.float32, 0.6, 1.2)
    noise = jnp.clip(jax.random.normal(key_noise, (ROWS, D), jnp.float32), -4.0, 4.0)
    values = mixing * base[owner] + noise
    return jnp.clip(values, -8.0, 8.0).astype(jnp.bfloat16)


def setup_inputs(seed: int = 0) -> dict:
    arg_keys = jax.random.split(jax.random.key(seed), 3)
    return {
        "passages": draw_passages(jax.random.fold_in(arg_keys[2], 71), 0),
        "centroids": draw_centroids(jax.random.fold_in(arg_keys[2], 71), 0),
    }


def unit(values):
    wide = values.astype(jnp.float32)
    return (wide * jax.lax.rsqrt(lax.optimization_barrier(jnp.sum(wide * wide, axis=-1, keepdims=True)) + 1e-06)).astype(jnp.bfloat16)

def reference(passages, centroids):
    row_unit = unit(passages)
    cent_unit = unit(centroids)
    kernel = jnp.exp(20.0 * jnp.dot(row_unit, cent_unit.T, preferred_element_type=jnp.float32))
    target = jnp.float32(ROWS / K)
    row_scale = jnp.ones((ROWS,), jnp.float32)
    col_scale = jnp.ones((K,), jnp.float32)
    for step in range(ITERS):
        col_scale = target / jnp.dot(row_scale, kernel)
        row_scale = 1.0 / jnp.dot(kernel, col_scale)
    plan = kernel * row_scale[:, None] * col_scale[None, :]
    list_mass = lax.optimization_barrier(jnp.sum(plan, axis=0))
    soft_sums = jnp.dot(plan.astype(jnp.bfloat16).T, row_unit, preferred_element_type=jnp.float32)
    return (soft_sums / list_mass[:, None], list_mass)
```

```python
import functools

import jax
import jax.numpy as jnp
from jax import lax
from jax.experimental import pallas as pl
from jax.experimental.pallas import tpu as pltpu
from jax.sharding import PartitionSpec as P

MESH = pl.DeviceIdType.MESH
F32 = jnp.float32
BF16 = jnp.bfloat16

ITERS = 3
D = 768
SIDE = 2048
OWN = 512
CHUNK = 128
GROUP = 256
SUB = 64
TILES = SIDE // 128
TARGET = 8.0
LOG2E20 = 20.0 * 1.4426950408889634

STAGES = (
    tuple((d, 0, e) for e in (0, 1) for d in range(4) if (d, e) != (0, 0)),
    tuple((0, d, 0) for d in (1, 2, 3)),
)
WIDEST = max(len(stage) for stage in STAGES)


def unit(values):
    wide = values.astype(F32)
    return (wide * lax.rsqrt(jnp.sum(wide * wide, axis=-1, keepdims=True) + 1e-06)).astype(BF16)


def spread(row):
    return jnp.broadcast_to(row, (128, 128)).T


def body(
    p_ref, cent_ref, out_ref, mass_ref,
    U, Us, C, K, Kb, csum, cb, colbuf, colrecv, rowbuf, rowrecv,
    Sb, Sr, Rl, Own, Tb, Tr, Tl, F4, Fs, Fr, wt, mbuf, mrecv,
    ag_s, ag_r, ps_s, ps_r, pz_s, pz_r, pf_s, pf_r, col_s, col_r, row_s, row_r,
    rs_s, rs_r, fin_s, fin_r, m_s, m_r,
):
    dp = lax.axis_index("dp")
    li = lax.axis_index("list")
    zl, c = dp // 2, dp % 2
    zh, x, y = li // 16, (li // 4) % 4, li % 4

    def dev(zh_, zl_, x_, y_, c_):
        return (zl_ * 2 + c_, zh_ * 16 + x_ * 4 + y_)

    sibling = dev(zh, zl, x, y, 1 - c)
    partner = dev(1 - zh, 1 - zl, x, y, c)
    partner_sibling = dev(1 - zh, 1 - zl, x, y, 1 - c)
    twin = dev(zh, 1 - zl, x, y, c)
    twin_sibling = dev(zh, 1 - zl, x, y, 1 - c)

    def near(dx, dy, dz):
        return dev(zh, (zl + dz) % 2, (x + dx) % 4, (y + dy) % 4, c)

    peers = [sibling, partner, partner_sibling, twin_sibling]
    for stage in STAGES:
        for delta in stage:
            peers.append(near(*delta))

    barrier = pltpu.get_barrier_semaphore()
    for peer in peers:
        pl.semaphore_signal(barrier, inc=1, device_id=peer, device_id_type=MESH)

    def remote(src, dst, send, recv, device):
        return pltpu.make_async_remote_copy(
            src_ref=src, dst_ref=dst, send_sem=send, recv_sem=recv,
            device_id=device, device_id_type=MESH,
        )

    def along(h, phase, step):
        if (h + phase) % 2 == 0:
            return near(step, 0, 0)
        return near(0, step, 0)

    def place(h, phase):
        return (x, y) if (h + phase) % 2 == 0 else (y, x)

    def ag_rows(h, phase, pos, half):
        if phase == 0:
            n = SUB
            at = h * 1024 + place(h, 0)[1] * GROUP + pos * SUB
        else:
            n = GROUP
            at = h * 1024 + pos * GROUP
        return C.at[pl.ds(pl.multiple_of(at + half * (n // 2), n // 2), n // 2), :]

    def ag_copy(h, phase, way, k, block):
        step = 1 if way == 0 else 3
        half = way if k != 1 else 1 - way
        ref = ag_rows(h, phase, block, half)
        return remote(ref, ref, ag_s.at[h, phase, way, k], ag_r.at[h, phase, way, k], along(h, phase, step))

    def ag_start(h, phase):
        me = place(h, phase)[0]
        for k in (0, 1):
            for way in (0, 1):
                ag_copy(h, phase, way, k, me).start()

    def behind(h, phase, way, k):
        me = place(h, phase)[0]
        if k == 2:
            return (me + 2) % 4
        return (me + (3 if way == 0 else 1)) % 4

    def ag_wait(h, phase, k):
        for way in (0, 1):
            ag_copy(h, phase, way, k, behind(h, phase, way, k)).wait_recv()

    def ag_relay(h, phase):
        for way in (0, 1):
            block = behind(h, phase, way, 0)
            ag_copy(h, phase, way, 0, block).wait_recv()
            ag_copy(h, phase, way, 2, block).start()

    def ag_drain(h, phase):
        me = place(h, phase)[0]
        for way in (0, 1):
            ag_copy(h, phase, way, 0, me).wait_send()
            ag_copy(h, phase, way, 1, me).wait_send()
            ag_copy(h, phase, way, 2, behind(h, phase, way, 0)).wait_send()

    for h in (0, 1):
        first, second = place(h, 0)
        at = pl.multiple_of(h * 1024 + second * GROUP + first * SUB, SUB)
        own = cent_ref[pl.ds(pl.multiple_of(c * 128 + h * SUB, SUB), SUB), :]
        C[pl.ds(at, SUB), :] = unit(own)

    pl.semaphore_wait(barrier, len(peers))
    for h in (0, 1):
        ag_start(h, 0)

    slot = zh * 2 + c
    slot_sib = zh * 2 + 1 - c
    slot_par = (1 - zh) * 2 + c
    slot_far = (1 - zh) * 2 + 1 - c

    def rows(which, k):
        return U.at[pl.ds(pl.multiple_of(which * OWN + k * CHUNK, CHUNK), CHUNK), :]

    def p_sib(which, k):
        return remote(rows(which, k), rows(which, k), ps_s.at[k], ps_r.at[k], sibling)

    def p_z(which, k):
        return remote(rows(which, k), rows(which, k), pz_s.at[k], pz_r.at[k], partner)

    def p_fwd(which, k):
        return remote(rows(which, k), rows(which, k), pf_s.at[k], pf_r.at[k], sibling)

    for k in range(OWN // CHUNK):
        U[pl.ds(pl.multiple_of(slot * OWN + k * CHUNK, CHUNK), CHUNK), :] = unit(
            p_ref[pl.ds(k * CHUNK, CHUNK), :]
        )
        p_z(slot, k).start()
        p_sib(slot, k).start()

    csum[...] = jnp.zeros_like(csum)

    def gemm1(g, q):
        at = pl.multiple_of(g * GROUP, GROUP)
        qt = pl.multiple_of(q * OWN, OWN)
        s = lax.dot_general(
            C[pl.ds(at, GROUP), :], U[pl.ds(qt, OWN), :],
            (((1,), (1,)), ((), ())), preferred_element_type=F32,
        )
        e = jnp.exp2(s * LOG2E20)
        K[pl.ds(at, GROUP), pl.ds(qt, OWN)] = e
        Kb[pl.ds(at, GROUP), pl.ds(qt, OWN)] = e.astype(BF16)
        part = e[:, 0:128] + e[:, 128:256] + (e[:, 256:384] + e[:, 384:512])
        csum[pl.ds(at, GROUP), :] += part

    for h in (0, 1):
        ag_relay(h, 0)
    for h in (0, 1):
        ag_wait(h, 0, 1)
        ag_wait(h, 0, 2)
        ag_start(h, 1)

    for k in range(OWN // CHUNK):
        p_sib(slot_sib, k).wait_recv()

    def forward(k):
        p_z(slot_par, k).wait_recv()
        p_fwd(slot_par, k).start()

    @pl.loop(0, 4)
    def _(i):
        h = i // 2
        gemm1(h * 4 + y * (1 - h) + x * h, zh * 2 + i % 2)

    forward(0)
    for h in (0, 1):
        ag_relay(h, 1)
    forward(1)
    for h in (0, 1):
        ag_wait(h, 1, 1)

    @pl.loop(0, 8)
    def _(i):
        h = i // 4
        pos = (y * (1 - h) + x * h + 1 + 2 * ((i // 2) % 2)) % 4
        gemm1(h * 4 + pos, zh * 2 + i % 2)

    forward(2)
    for h in (0, 1):
        ag_wait(h, 1, 2)

    @pl.loop(0, 4)
    def _(i):
        h = i // 2
        pos = (y * (1 - h) + x * h + 2) % 4
        gemm1(h * 4 + pos, zh * 2 + i % 2)

    forward(3)

    @pl.loop(0, 8)
    def _(g):
        gemm1(g, slot_par)

    for k in range(OWN // CHUNK):
        p_fwd(slot_far, k).wait_recv()

    @pl.loop(0, 8)
    def _(g):
        gemm1(g, slot_far)

    def col_pass(r16):
        r = [jnp.broadcast_to(r16[t : t + 1, :], (8, 128)) for t in range(TILES)]

        @pl.loop(0, SIDE // 64)
        def _(i):
            for s in range(8):
                at = pl.multiple_of(i * 64 + s * 8, 8)
                acc = [None] * 4
                for t in range(TILES):
                    term = K[pl.ds(at, 8), t * 128 : (t + 1) * 128] * r[t]
                    acc[t % 4] = term if acc[t % 4] is None else acc[t % 4] + term
                csum[pl.ds(at, 8), :] = (acc[0] + acc[1]) + (acc[2] + acc[3])

    def fold():
        parts = []
        for b in range(TILES):
            block = csum[b * 128 : (b + 1) * 128, :]
            parts.append(jnp.sum(block.T, axis=0, keepdims=True))
        return jnp.concatenate(parts, axis=0)

    def col_copy(it, st, k):
        return remote(
            colbuf.at[it, st], colrecv.at[it, st, k], col_s.at[st, k], col_r.at[it, st, k],
            near(*STAGES[st][k]),
        )

    def col_send(it, st, value):
        colbuf[it, st] = value
        for k in range(len(STAGES[st])):
            col_copy(it, st, k).start()

    def col_take(it, st):
        total = colbuf[it, st]
        for k in range(len(STAGES[st])):
            col_copy(it, st, k).wait_recv()
            total += colrecv[it, st, k]
        for k in range(len(STAGES[st])):
            col_copy(it, st, k).wait_send()
        return total

    def row_pass():
        def step(i, acc):
            acc = list(acc)
            for s in range(4):
                at = pl.multiple_of(i * 32 + s * 8, 8)
                scale = cb[pl.ds(at, 8), :]
                for t in range(TILES):
                    acc[t] += K[pl.ds(at, 8), t * 128 : (t + 1) * 128] * scale
            return tuple(acc)

        zero = tuple(jnp.zeros((8, 128), F32) for _ in range(TILES))
        acc = lax.fori_loop(0, SIDE // 32, step, zero)
        return jnp.concatenate([jnp.sum(a, axis=0, keepdims=True) for a in acc], axis=0)

    row_peers = (sibling, partner, partner_sibling)

    def row_copy(it, k):
        return remote(rowbuf.at[it], rowrecv.at[it, k], row_s.at[k], row_r.at[it, k], row_peers[k])

    def row_sum(it, value):
        rowbuf[it] = value
        for k in range(3):
            row_copy(it, k).start()
        total = value
        for k in range(3):
            row_copy(it, k).wait_recv()
            total += rowrecv[it, k]
        for k in range(3):
            row_copy(it, k).wait_send()
        return total

    r16 = None
    for it in range(ITERS):
        if it > 0:
            col_pass(r16)
        col_send(it, 0, fold())
        col_send(it, 1, col_take(it, 0))
        c16 = TARGET / col_take(it, 1)
        for b in range(TILES):
            cb[b * 128 : (b + 1) * 128, :] = spread(c16[b : b + 1, :])
        r16 = 1.0 / row_sum(it, row_pass())

    col_pass(r16)
    col_send(ITERS, 0, fold())

    for b in range(TILES):
        scale = spread(r16[b : b + 1, :])
        wide = U[b * 128 : (b + 1) * 128, :].astype(F32)
        Us[b * 128 : (b + 1) * 128, :] = (
            wide * jnp.concatenate([scale] * (D // 128), axis=1)
        ).astype(BF16)

    def gemm2(g):
        at = pl.multiple_of(g * GROUP, GROUP)
        return jnp.dot(Kb[pl.ds(at, GROUP), :], Us[...], preferred_element_type=F32)

    def rs_bufs(phase):
        return (Sb, Sr, Rl, GROUP) if phase == 1 else (Tb, Tr, Tl, SUB)

    def rs_copy(h, phase, way, k):
        sb, sr, rl, n = rs_bufs(phase)
        step = 1 if way == 0 else 3
        m = n // 2
        if k == 0:
            src, dst = sb.at[h, 2, pl.ds(way * m, m), :], rl.at[h, way]
        else:
            half = 1 - way if k == 1 else way
            src, dst = sb.at[h, way, pl.ds(half * m, m), :], sr.at[h, way, pl.ds(half * m, m), :]
        return remote(src, dst, rs_s.at[h, phase, way, k], rs_r.at[h, phase, way, k], along(h, phase, step))

    def rs_far(h, phase, value):
        sb = rs_bufs(phase)[0]
        sb[h, 2] = value.astype(BF16)
        for way in (0, 1):
            rs_copy(h, phase, way, 0).start()

    def rs_near(h, phase, way, value):
        sb, sr, rl, n = rs_bufs(phase)
        m = n // 2
        other = 1 - way
        sb[h, way, pl.ds(other * m, m), :] = value[other * m : (other + 1) * m, :].astype(BF16)
        rs_copy(h, phase, way, 1).start()
        rs_copy(h, phase, way, 0).wait_recv()
        sb[h, way, pl.ds(way * m, m), :] = (
            value[way * m : (way + 1) * m, :] + rl[h, way].astype(F32)
        ).astype(BF16)
        rs_copy(h, phase, way, 2).start()

    def rs_take(h, phase, value):
        sr = rs_bufs(phase)[1]
        for way in (0, 1):
            for k in (1, 2):
                rs_copy(h, phase, way, k).wait_recv()
        return value + sr[h, 0].astype(F32) + sr[h, 1].astype(F32)

    def rs_drain(h, phase):
        for way in (0, 1):
            for k in (0, 1, 2):
                rs_copy(h, phase, way, k).wait_send()

    def group(h, step):
        return h * 4 + (place(h, 1)[0] + step) % 4

    for h in (0, 1):
        rs_far(h, 1, gemm2(group(h, 2)))
    col_send(ITERS, 1, col_take(ITERS, 0))
    for way, step in ((0, 1), (1, 3)):
        for h in (0, 1):
            rs_near(h, 1, way, gemm2(group(h, step)))
    for h in (0, 1):
        Own[h] = gemm2(group(h, 0))
    wbuf = mbuf
    colbuf[ITERS, 1] = col_take(ITERS, 1)
    for h in (0, 1):
        first, second = place(h, 0)
        block = h * 8 + second * 2 + first // 2
        wt[...] = spread(colbuf[ITERS, 1, pl.ds(block, 1), :])
        wbuf[pl.ds(h * SUB, SUB), :] = wt[pl.ds(pl.multiple_of((first % 2) * SUB, SUB), SUB), :]
        at = pl.multiple_of(h * 1024 + second * GROUP + first * SUB, SUB)
        wt[pl.ds(0, SUB), :] = cb[pl.ds(at, SUB), :]
        mrecv[0, pl.ds(h * SUB, SUB), :] = wbuf[pl.ds(h * SUB, SUB), :] * wt[pl.ds(0, SUB), :]
    mass = mrecv[0].T[0:8, :]
    mrecv[1, pl.ds(0, 8), :] = mass
    mass_copy = remote(mrecv.at[1, pl.ds(0, 8), :], mrecv.at[1, pl.ds(8, 8), :], m_s.at[0], m_r.at[0], sibling)
    mass_copy.start()

    for h in (0, 1):
        Own[h] = rs_take(h, 1, Own[h])

    def sub(h, step):
        me = place(h, 0)[0]
        return Own[h, pl.ds(pl.multiple_of(((me + step) % 4) * SUB, SUB), SUB), :]

    for h in (0, 1):
        rs_far(h, 0, sub(h, 2))
    for way, step in ((0, 1), (1, 3)):
        for h in (0, 1):
            rs_near(h, 0, way, sub(h, step))
    for h in (0, 1):
        total = rs_take(h, 0, sub(h, 0))
        weight = wbuf[pl.ds(h * SUB, SUB), :]
        total = total * jnp.concatenate([1.0 / weight] * (D // 128), axis=1)
        for k in range(4):
            piece = total[:, k * 192 : (k + 1) * 192]
            F4[k, pl.ds(h * SUB, SUB), :] = piece
            Fs[k, pl.ds(h * SUB, SUB), :] = piece.astype(BF16)

    fin_peers = (
        (twin, (1 - zl) * 2 + c),
        (sibling, zl * 2 + 1 - c),
        (twin_sibling, (1 - zl) * 2 + 1 - c),
    )

    def fin_copy(k):
        return remote(Fs.at[fin_peers[k][1]], Fr.at[k], fin_s.at[k], fin_r.at[k], fin_peers[k][0])

    for k in (2, 0, 1):
        fin_copy(k).start()
    mass_copy.wait_recv()
    mass_ref[pl.ds(c, 1), :] = mrecv[1, pl.ds(0, 1), :]
    mass_ref[pl.ds(1 - c, 1), :] = mrecv[1, pl.ds(8, 1), :]
    fin_copy(0).wait_recv()
    out_ref[pl.ds(pl.multiple_of(c * 128, 128), 128), :] = F4[dp] + Fr[0].astype(F32)
    fin_copy(1).wait_recv()
    fin_copy(2).wait_recv()
    out_ref[pl.ds(pl.multiple_of((1 - c) * 128, 128), 128), :] = Fr[1].astype(F32) + Fr[2].astype(F32)

    for h in (0, 1):
        for phase in (0, 1):
            ag_drain(h, phase)
            rs_drain(h, phase)
    for k in range(OWN // CHUNK):
        p_z(slot, k).wait_send()
        p_sib(slot, k).wait_send()
        p_fwd(slot_par, k).wait_send()
    mass_copy.wait_send()
    for k in range(3):
        fin_copy(k).wait_send()


def on_device(passages, centroids):
    lists = centroids.shape[0]
    width = D // 4
    chunks = OWN // CHUNK
    dma = pltpu.SemaphoreType.DMA
    vm = pltpu.VMEM
    new, mass = pl.pallas_call(
        body,
        out_shape=(
            jax.ShapeDtypeStruct((lists, width), F32),
            jax.ShapeDtypeStruct((2, 128), F32),
        ),
        in_specs=[pl.BlockSpec(memory_space=pltpu.VMEM)] * 2,
        out_specs=(pl.BlockSpec(memory_space=pltpu.VMEM),) * 2,
        scratch_shapes=[
            vm((SIDE, D), BF16),
            vm((SIDE, D), BF16),
            vm((SIDE, D), BF16),
            vm((SIDE, SIDE), F32),
            vm((SIDE, SIDE), BF16),
            vm((SIDE, 128), F32),
            vm((SIDE, 128), F32),
            vm((ITERS + 1, 2, TILES, 128), F32),
            vm((ITERS + 1, 2, WIDEST, TILES, 128), F32),
            vm((ITERS, TILES, 128), F32),
            vm((ITERS, 3, TILES, 128), F32),
            vm((2, 3, GROUP, D), BF16),
            vm((2, 2, GROUP, D), BF16),
            vm((2, 2, GROUP // 2, D), BF16),
            vm((2, GROUP, D), F32),
            vm((2, 3, SUB, D), BF16),
            vm((2, 2, SUB, D), BF16),
            vm((2, 2, SUB // 2, D), BF16),
            vm((4, 128, width), F32),
            vm((4, 128, width), BF16),
            vm((3, 128, width), BF16),
            vm((128, 128), F32),
            vm((128, 128), F32),
            vm((2, 128, 128), F32),
            dma((2, 2, 2, 3)), dma((2, 2, 2, 3)),
            dma((chunks,)), dma((chunks,)),
            dma((chunks,)), dma((chunks,)),
            dma((chunks,)), dma((chunks,)),
            dma((2, WIDEST)), dma((ITERS + 1, 2, WIDEST)),
            dma((3,)), dma((ITERS, 3)),
            dma((2, 2, 2, 3)), dma((2, 2, 2, 3)),
            dma((3,)), dma((3,)),
            dma((1,)), dma((1,)),
        ],
        compiler_params=pltpu.CompilerParams(
            collective_id=0, has_side_effects=True, vmem_limit_bytes=60 * 1024 * 1024
        ),
        cost_estimate=pl.CostEstimate(
            flops=4 * SIDE * SIDE * D, bytes_accessed=2 * 1024 * 1024, transcendentals=SIDE * SIDE
        ),
        name="sinkhorn",
    )(passages, centroids)
    return new, mass.reshape(lists)


def solution(mesh):
    return jax.shard_map(
        on_device,
        mesh=mesh,
        in_specs=(P(("dp", "list"), None), P("list", None)),
        out_specs=(P("list", "dp"), P("list")),
        check_vma=False,
    )
```

```python
import jax
import jax.numpy as jnp
from jax import lax
from jax.experimental import pallas as pl
from jax.experimental.pallas import tpu as pltpu
from jax.sharding import PartitionSpec as P

MESH = pl.DeviceIdType.MESH
F32 = jnp.float32
BF16 = jnp.bfloat16

ITERS = 3
D = 768
SIDE = 2048
OWN = 512
CHUNK = 128
GROUP = 256
SUB = 64
TILES = SIDE // 128
TARGET = 8.0
LOG2E20 = 20.0 * 1.4426950408889634

WIDTH = D // 4
WAVE = D // 2


def far_first():
    deltas = [(a, b, e) for a in range(4) for b in range(4) for e in (0, 1) if (a, b, e) != (0, 0, 0)]
    return tuple(sorted(deltas, key=lambda d: -(min(d[0], 4 - d[0]) + min(d[1], 4 - d[1]) + d[2])))


PEERS = far_first()


def unit(values):
    wide = values.astype(F32)
    return (wide * lax.rsqrt(jnp.sum(wide * wide, axis=-1, keepdims=True) + 1e-06)).astype(BF16)


def spread(row):
    return jnp.broadcast_to(row, (128, 128)).T


def body(
    p_hbm, cent_hbm, out_ref, mass_ref,
    P_in, C_in, U, Us, C, K, Kb, csum, cb, colbuf, colrecv, rowbuf, rowrecv,
    Sb, Sr, Rl, Acc, Own, Tb, Tr, Fs, Fr, wt, wbuf, mbuf,
    in_s, a0_s, a0_r, a1_s, a1_r, ps_s, ps_r, pz_s, pz_r, pf_s, pf_r, col_s, col_r, row_s, row_r,
    rs_s, rs_r, r2_s, r2_r, fin_s, fin_r, m_s, m_r,
):
    dp = lax.axis_index("dp")
    li = lax.axis_index("list")
    zl, c = dp // 2, dp % 2
    zh, x, y = li // 16, (li // 4) % 4, li % 4

    def dev(zh_, zl_, x_, y_, c_):
        return (zl_ * 2 + c_, zh_ * 16 + x_ * 4 + y_)

    sibling = dev(zh, zl, x, y, 1 - c)
    partner = dev(1 - zh, 1 - zl, x, y, c)
    partner_sibling = dev(1 - zh, 1 - zl, x, y, 1 - c)
    twin = dev(zh, 1 - zl, x, y, c)
    twin_sibling = dev(zh, 1 - zl, x, y, 1 - c)

    def near(dx, dy, dz):
        return dev(zh, (zl + dz) % 2, (x + dx) % 4, (y + dy) % 4, c)

    peers = [near(*delta) for delta in PEERS] + [partner_sibling, partner, twin_sibling, sibling]
    barrier = pltpu.get_barrier_semaphore()
    for peer in peers:
        pl.semaphore_signal(barrier, inc=1, device_id=peer, device_id_type=MESH)

    def remote(src, dst, send, recv, device):
        return pltpu.make_async_remote_copy(
            src_ref=src, dst_ref=dst, send_sem=send, recv_sem=recv,
            device_id=device, device_id_type=MESH,
        )

    p_in = pltpu.make_async_copy(p_hbm, P_in, in_s.at[0])
    c_in = pltpu.make_async_copy(cent_hbm.at[pl.ds(pl.multiple_of(c * 128, 128), 128), :], C_in, in_s.at[1])
    p_in.start()
    c_in.start()

    def along(h, phase, step):
        if (h + phase) % 2 == 0:
            return near(step, 0, 0)
        return near(0, step, 0)

    def place(h, phase):
        return (x, y) if (h + phase) % 2 == 0 else (y, x)

    def block(h, a, b, part, parts):
        n = SUB // parts
        at = h * 1024 + b * GROUP + a * SUB + part * n
        return C.at[pl.ds(pl.multiple_of(at, n), n), :]

    def a0_copy(h, d, sent=True):
        a, b = place(h, 0)
        ref = block(h, a if sent else (a + 4 - d) % 4, b, 0, 1)
        return remote(ref, ref, a0_s.at[h, d - 1], a0_r.at[h, d - 1], along(h, 0, d))

    def a1_copy(h, j, way, k, sent=True):
        a, b = place(h, 0)
        back = (3 if way == 0 else 1)
        src = b if sent else (b + back) % 4
        if k == 2:
            src = (b + (back if sent else 2)) % 4
        half = way if k != 1 else 1 - way
        ref = block(h, (a + 4 - j) % 4, src, half, 2)
        return remote(
            ref, ref, a1_s.at[h, j, way, k], a1_r.at[h, j, way, k], along(h, 1, 1 if way == 0 else 3)
        )

    def a1_start(j):
        for k in (0, 1):
            for h in (0, 1):
                for way in (0, 1):
                    a1_copy(h, j, way, k).start()

    def a1_relay(j):
        for h in (0, 1):
            for way in (0, 1):
                a1_copy(h, j, way, 0, False).wait_recv()
                a1_copy(h, j, way, 2).start()

    def a1_wait(j, k):
        for h in (0, 1):
            for way in (0, 1):
                a1_copy(h, j, way, k, False).wait_recv()

    def rows(zh_, k, core):
        return pl.ds(pl.multiple_of(zh_ * 1024 + k * 256 + core * CHUNK, CHUNK), CHUNK)

    chunks = OWN // CHUNK

    def p_copy(zh_, core, k, send, recv, device):
        ref = U.at[rows(zh_, k, core), :]
        return remote(ref, ref, send.at[k], recv.at[k], device)

    def p_z(k, sent=True):
        return p_copy(zh if sent else 1 - zh, c, k, pz_s, pz_r, partner)

    def p_sib(k, sent=True):
        return p_copy(zh, c if sent else 1 - c, k, ps_s, ps_r, sibling)

    def p_fwd(k, sent=True):
        return p_copy(1 - zh, c if sent else 1 - c, k, pf_s, pf_r, sibling)

    def forward(k):
        p_z(k, False).wait_recv()
        p_fwd(k).start()

    p_in.wait()
    for k in range(chunks):
        U[rows(zh, k, c), :] = unit(P_in[pl.ds(k * CHUNK, CHUNK), :])
    c_in.wait()
    for h in (0, 1):
        a, b = place(h, 0)
        at = pl.multiple_of(h * 1024 + b * GROUP + a * SUB, SUB)
        C[pl.ds(at, SUB), :] = unit(C_in[pl.ds(h * SUB, SUB), :])

    pl.semaphore_wait(barrier, len(peers))
    for h in (0, 1):
        for d in (1, 3):
            a0_copy(h, d).start()
    p_z(0).start()
    for h in (0, 1):
        a0_copy(h, 2).start()
    p_sib(0).start()
    a1_start(0)
    for k in range(1, chunks):
        p_z(k).start()
        p_sib(k).start()

    def gemm1(at, m, qt, n, first):
        s = lax.dot_general(
            C[pl.ds(at, m), :], U[pl.ds(qt, n), :],
            (((1,), (1,)), ((), ())), preferred_element_type=F32,
        )
        e = jnp.exp2(s * LOG2E20)
        K[pl.ds(at, m), pl.ds(qt, n)] = e
        Kb[pl.ds(at, m), pl.ds(qt, n)] = e.astype(BF16)
        part = [e[:, t * 128 : (t + 1) * 128] for t in range(n // 128)]
        while len(part) > 1:
            part = [part[t] + part[t + 1] for t in range(0, len(part), 2)]
        csum[pl.ds(at, m), :] = part[0] if first else csum[pl.ds(at, m), :] + part[0]

    own_rows = pl.multiple_of(zh * 1024, 1024)
    far_rows = pl.multiple_of((1 - zh) * 1024, 1024)

    def own_gemm(step):
        @pl.loop(0, 2)
        def _(h):
            pos = (y * (1 - h) + x * h + step) % 4
            gemm1(pl.multiple_of(h * 1024 + pos * GROUP, GROUP), GROUP, own_rows, 1024, True)

    def far_gemm(k):
        gemm1(0, SIDE, pl.multiple_of(far_rows + k * 256, 256), 256, False)

    for d in (1, 3):
        for h in (0, 1):
            a0_copy(h, d, False).wait_recv()
        a1_start(d)
    for h in (0, 1):
        a0_copy(h, 2, False).wait_recv()
    a1_start(2)
    a1_relay(0)
    for k in range(chunks):
        p_sib(k, False).wait_recv()
    own_gemm(0)
    a1_relay(1)
    forward(0)
    a1_relay(3)
    a1_relay(2)
    for j in (0, 1, 3, 2):
        a1_wait(j, 1)
    own_gemm(1)
    forward(1)
    own_gemm(3)
    for j in (0, 1, 3, 2):
        a1_wait(j, 2)
    own_gemm(2)
    p_fwd(0, False).wait_recv()
    far_gemm(0)
    forward(2)
    p_fwd(1, False).wait_recv()
    far_gemm(1)
    p_fwd(2, False).wait_recv()
    far_gemm(2)
    forward(3)
    p_fwd(3, False).wait_recv()
    far_gemm(3)

    def col_pass(r16):
        r = [jnp.broadcast_to(r16[t : t + 1, :], (8, 128)) for t in range(TILES)]

        @pl.loop(0, SIDE // 64)
        def _(i):
            for s in range(8):
                at = pl.multiple_of(i * 64 + s * 8, 8)
                acc = [None] * 4
                for t in range(TILES):
                    term = K[pl.ds(at, 8), t * 128 : (t + 1) * 128] * r[t]
                    acc[t % 4] = term if acc[t % 4] is None else acc[t % 4] + term
                csum[pl.ds(at, 8), :] = (acc[0] + acc[1]) + (acc[2] + acc[3])

    def fold():
        parts = []
        for b in range(TILES):
            square = csum[b * 128 : (b + 1) * 128, :]
            parts.append(jnp.sum(square.T, axis=0, keepdims=True))
        return jnp.concatenate(parts, axis=0)

    def col_send(it, value):
        colbuf[it] = value
        for k, delta in enumerate(PEERS):
            remote(colbuf.at[it], colrecv.at[it, k], col_s.at[it], col_r.at[it], near(*delta)).start()

    def col_all(it):
        return remote(colrecv.at[it], colrecv.at[it], col_s.at[it], col_r.at[it], near(*PEERS[0]))

    def col_take(it):
        col_all(it).wait_recv()
        return jnp.sum(colrecv[it], axis=0) + colbuf[it]

    def row_pass():
        def step(i, acc):
            acc = list(acc)
            for s in range(4):
                at = pl.multiple_of(i * 32 + s * 8, 8)
                scale = cb[pl.ds(at, 8), :]
                for t in range(TILES):
                    acc[t] += K[pl.ds(at, 8), t * 128 : (t + 1) * 128] * scale
            return tuple(acc)

        zero = tuple(jnp.zeros((8, 128), F32) for _ in range(TILES))
        acc = lax.fori_loop(0, SIDE // 32, step, zero)
        return jnp.concatenate([jnp.sum(a, axis=0, keepdims=True) for a in acc], axis=0)

    row_peers = (partner_sibling, partner, sibling)

    def row_copy(it, k):
        return remote(rowbuf.at[it], rowrecv.at[it, k], row_s.at[it, k], row_r.at[it, k], row_peers[k])

    def row_sum(it, value):
        rowbuf[it] = value
        for k in range(3):
            row_copy(it, k).start()
        total = value
        for k in (2, 1, 0):
            row_copy(it, k).wait_recv()
            total += rowrecv[it, k]
        return total

    r16 = None
    for it in range(ITERS):
        if it > 0:
            col_pass(r16)
        col_send(it, fold())
        c16 = TARGET / col_take(it)
        for b in range(TILES):
            cb[b * 128 : (b + 1) * 128, :] = spread(c16[b : b + 1, :])
        r16 = 1.0 / row_sum(it, row_pass())

    for b in range(TILES):
        scale = spread(r16[b : b + 1, :])
        wide = U[b * 128 : (b + 1) * 128, :].astype(F32)
        Us[b * 128 : (b + 1) * 128, :] = (
            wide * jnp.concatenate([scale] * (D // 128), axis=1)
        ).astype(BF16)

    def gemm2(h, step):
        at = pl.multiple_of(h * 1024 + (place(h, 1)[0] + step) % 4 * GROUP, GROUP)
        return jnp.dot(Kb[pl.ds(at, GROUP), :], Us[...], preferred_element_type=F32)

    HALF = GROUP // 2

    def cols(w):
        return slice(w * WAVE, (w + 1) * WAVE)

    def rs_copy(h, w, way, k):
        lanes = pl.ds(w * WAVE, WAVE)
        if k == 0:
            src, dst = Sb.at[h, 2, pl.ds(way * HALF, HALF), lanes], Rl.at[h, way, :, lanes]
        else:
            half = 1 - way if k == 1 else way
            src, dst = (b.at[h, way, pl.ds(half * HALF, HALF), lanes] for b in (Sb, Sr))
        return remote(
            src, dst, rs_s.at[h, w, way, k], rs_r.at[h, w, way, k], along(h, 1, 1 if way == 0 else 3)
        )

    def rs_add(h, w, way):
        half = pl.ds(way * HALF, HALF)
        rs_copy(h, w, way, 0).wait_recv()
        Sb[h, way, half, cols(w)] = (Acc[h, way, :, cols(w)] + Rl[h, way, :, cols(w)].astype(F32)).astype(BF16)
        rs_copy(h, w, way, 2).start()

    for h in (0, 1):
        Sb[h, 2] = gemm2(h, 2).astype(BF16)
        for w in (0, 1):
            for way in (0, 1):
                rs_copy(h, w, way, 0).start()

    col_pass(r16)
    col_send(ITERS, fold())

    for way, step in ((0, 1), (1, 3)):
        for h in (0, 1):
            value = gemm2(h, step)
            other = 1 - way
            Sb[h, way, pl.ds(other * HALF, HALF), :] = value[other * HALF : (other + 1) * HALF, :].astype(BF16)
            Acc[h, way] = value[way * HALF : (way + 1) * HALF, :]
            rs_copy(h, 0, way, 1).start()
            rs_add(h, 0, way)
            rs_copy(h, 1, way, 1).start()
    for h in (0, 1):
        Own[h] = gemm2(h, 0)
    for way in (0, 1):
        for h in (0, 1):
            rs_add(h, 1, way)

    mass16 = col_take(ITERS)
    colbuf[ITERS + 1] = mass16
    for h in (0, 1):
        a, b = place(h, 0)
        mine = pl.ds(h * SUB, SUB)
        wt[...] = spread(colbuf[ITERS + 1, pl.ds(h * 8 + b * 2 + a // 2, 1), :])
        wbuf[mine, :] = wt[pl.ds(pl.multiple_of((a % 2) * SUB, SUB), SUB), :]
        scale = cb[pl.ds(pl.multiple_of(h * 1024 + b * GROUP + a * SUB, SUB), SUB), :]
        wt[mine, :] = wbuf[mine, :] * scale
        if h == 0:
            held = wt[mine, :]
    mass = jnp.concatenate([held, wt[pl.ds(SUB, SUB), :]], axis=0).T[0:8, :]
    mbuf[0] = mass
    mass_copy = remote(mbuf.at[0], mbuf.at[1], m_s.at[0], m_r.at[0], sibling)
    mass_copy.start()

    def r2_copy(h, w, d):
        lanes = pl.ds(w * WAVE, WAVE)
        return remote(
            Tb.at[h, d - 1, :, lanes], Tr.at[h, d - 1, :, lanes],
            r2_s.at[h, w, d - 1], r2_r.at[h, w, d - 1], along(h, 0, d),
        )

    def sub(h, d):
        return pl.ds(pl.multiple_of((place(h, 0)[0] + d) % 4 * SUB, SUB), SUB)

    for w in (0, 1):
        for h in (0, 1):
            for way in (0, 1):
                for k in (1, 2):
                    rs_copy(h, w, way, k).wait_recv()
            Own[h, :, cols(w)] += Sr[h, 0, :, cols(w)].astype(F32) + Sr[h, 1, :, cols(w)].astype(F32)
            for d in (2, 1, 3):
                Tb[h, d - 1, :, cols(w)] = Own[h, sub(h, d), cols(w)].astype(BF16)
                r2_copy(h, w, d).start()

    fin_peers = (
        (twin, (1 - zl) * 2 + c),
        (sibling, zl * 2 + 1 - c),
        (twin_sibling, (1 - zl) * 2 + 1 - c),
    )

    def fin_copy(k):
        return remote(Fs.at[fin_peers[k][1]], Fr.at[k], fin_s.at[k], fin_r.at[k], fin_peers[k][0])

    for w in (0, 1):
        for h in (0, 1):
            total = Own[h, sub(h, 0), cols(w)]
            for d in (2, 1, 3):
                r2_copy(h, w, d).wait_recv()
                total += Tr[h, d - 1, :, cols(w)].astype(F32)
            weight = 1.0 / wbuf[pl.ds(h * SUB, SUB), :]
            total *= jnp.concatenate([weight] * (WAVE // 128), axis=1)
            Own[h, sub(h, 0), cols(w)] = total
            for k in (0, 1):
                Fs[2 * w + k, pl.ds(h * SUB, SUB), :] = total[:, k * WIDTH : (k + 1) * WIDTH].astype(BF16)
    for k in (2, 0, 1):
        fin_copy(k).start()

    mass_copy.wait_recv()
    mass_ref[0:1, :] = mbuf[c, 0:1, :]
    mass_ref[1:2, :] = mbuf[1 - c, 0:1, :]

    def turned(value):
        return jnp.concatenate(
            [value[:, 0:128].T, jnp.concatenate([value[:, 128:192], jnp.zeros((128, 64), F32)], axis=1).T[0:64, :]],
            axis=0,
        )

    mine = jnp.concatenate([Own[h, sub(h, 0), :] for h in (0, 1)], axis=0)
    own_piece = mine[:, 0:WIDTH]
    for k in (1, 2, 3):
        own_piece = jnp.where(dp == k, mine[:, k * WIDTH : (k + 1) * WIDTH], own_piece)
    fin_copy(1).wait_recv()
    fin_copy(0).wait_recv()
    fin_copy(2).wait_recv()
    out_ref[:, pl.ds(pl.multiple_of(c * 128, 128), 128)] = turned(own_piece + Fr[0].astype(F32))
    out_ref[:, pl.ds(pl.multiple_of((1 - c) * 128, 128), 128)] = turned(Fr[1].astype(F32) + Fr[2].astype(F32))

    for h in (0, 1):
        for d in (1, 2, 3):
            a0_copy(h, d).wait_send()
            for w in (0, 1):
                r2_copy(h, w, d).wait_send()
        for way in (0, 1):
            for k in (0, 1, 2):
                for j in range(4):
                    a1_copy(h, j, way, k).wait_send()
                for w in (0, 1):
                    rs_copy(h, w, way, k).wait_send()
    for k in range(chunks):
        p_z(k).wait_send()
        p_sib(k).wait_send()
        p_fwd(k).wait_send()
    for it in range(ITERS + 1):
        col_all(it).wait_send()
    for it in range(ITERS):
        for k in range(3):
            row_copy(it, k).wait_send()
    mass_copy.wait_send()
    for k in range(3):
        fin_copy(k).wait_send()


def on_device(passages, centroids):
    lists = centroids.shape[0]
    chunks = OWN // CHUNK
    dma = pltpu.SemaphoreType.DMA
    vm = pltpu.VMEM
    new, mass = pl.pallas_call(
        body,
        out_shape=(
            jax.ShapeDtypeStruct((WIDTH, lists), F32),
            jax.ShapeDtypeStruct((2, 128), F32),
        ),
        in_specs=[pl.BlockSpec(memory_space=pl.ANY)] * 2,
        out_specs=(pl.BlockSpec(memory_space=pltpu.VMEM),) * 2,
        scratch_shapes=[
            vm((OWN, D), BF16),
            vm((128, D), BF16),
            vm((SIDE, D), BF16),
            vm((SIDE, D), BF16),
            vm((SIDE, D), BF16),
            vm((SIDE, SIDE), F32),
            vm((SIDE, SIDE), BF16),
            vm((SIDE, 128), F32),
            vm((SIDE, 128), F32),
            vm((ITERS + 2, TILES, 128), F32),
            vm((ITERS + 1, len(PEERS), TILES, 128), F32),
            vm((ITERS, TILES, 128), F32),
            vm((ITERS, 3, TILES, 128), F32),
            vm((2, 3, GROUP, D), BF16),
            vm((2, 2, GROUP, D), BF16),
            vm((2, 2, GROUP // 2, D), BF16),
            vm((2, 2, GROUP // 2, D), F32),
            vm((2, GROUP, D), F32),
            vm((2, 3, SUB, D), BF16),
            vm((2, 3, SUB, D), BF16),
            vm((4, 128, WIDTH), BF16),
            vm((3, 128, WIDTH), BF16),
            vm((128, 128), F32),
            vm((128, 128), F32),
            vm((2, 8, 128), F32),
            dma((2,)),
            dma((2, 3)), dma((2, 3)),
            dma((2, 4, 2, 3)), dma((2, 4, 2, 3)),
            dma((chunks,)), dma((chunks,)),
            dma((chunks,)), dma((chunks,)),
            dma((chunks,)), dma((chunks,)),
            dma((ITERS + 1,)), dma((ITERS + 1,)),
            dma((ITERS, 3)), dma((ITERS, 3)),
            dma((2, 2, 2, 3)), dma((2, 2, 2, 3)),
            dma((2, 2, 3)), dma((2, 2, 3)),
            dma((3,)), dma((3,)),
            dma((1,)), dma((1,)),
        ],
        compiler_params=pltpu.CompilerParams(
            collective_id=0, has_side_effects=True, vmem_limit_bytes=60 * 1024 * 1024
        ),
        cost_estimate=pl.CostEstimate(
            flops=4 * SIDE * SIDE * D, bytes_accessed=2 * 1024 * 1024, transcendentals=SIDE * SIDE
        ),
        name="sinkhorn",
    )(passages, centroids)
    return new.T, mass.reshape(lists)


def solution(mesh):
    return jax.shard_map(
        on_device,
        mesh=mesh,
        in_specs=(P(("dp", "list"), None), P("list", None)),
        out_specs=(P("list", "dp"), P("list")),
        check_vma=False,
    )
```

```python
import jax
import jax.numpy as jnp
from jax import lax
from jax.experimental import pallas as pl
from jax.experimental.pallas import tpu as pltpu
from jax.sharding import PartitionSpec as P

MESH = pl.DeviceIdType.MESH
F32 = jnp.float32
BF16 = jnp.bfloat16

ITERS = 3
D = 768
SIDE = 2048
OWN = 512
CHUNK = 128
GROUP = 256
SUB = 64
TILES = SIDE // 128
TARGET = 8.0
LOG2E20 = 20.0 * 1.4426950408889634

WIDTH = D // 4
WAVE = D // 2


def far_first():
    deltas = [(a, b, e) for a in range(4) for b in range(4) for e in (0, 1) if (a, b, e) != (0, 0, 0)]
    return tuple(sorted(deltas, key=lambda d: -(min(d[0], 4 - d[0]) + min(d[1], 4 - d[1]) + d[2])))


PEERS = far_first()


def unit(values):
    wide = values.astype(F32)
    return (wide * lax.rsqrt(jnp.sum(wide * wide, axis=-1, keepdims=True) + 1e-06)).astype(BF16)


def spread(row):
    return jnp.broadcast_to(row, (128, 128)).T


def body(
    p_hbm, cent_hbm, out_ref, mass_ref,
    P_in, C_in, U, Us, C, K, Kb, csum, cb, colbuf, colrecv, rowbuf, rowrecv,
    Sb, Sr, Rl, Acc, Own, Tb, Tr, Fs, Fr, wt, wbuf, mbuf,
    in_s, a0_s, a0_r, a1_s, a1_r, ps_s, ps_r, pz_s, pz_r, pf_s, pf_r, col_s, col_r, row_s, row_r,
    rs_s, rs_r, r2_s, r2_r, fin_s, fin_r, m_s, m_r, ready,
):
    dp = lax.axis_index("dp")
    li = lax.axis_index("list")
    zl, c = dp // 2, dp % 2
    zh, x, y = li // 16, (li // 4) % 4, li % 4

    def dev(zh_, zl_, x_, y_, c_):
        return (zl_ * 2 + c_, zh_ * 16 + x_ * 4 + y_)

    sibling = dev(zh, zl, x, y, 1 - c)
    partner = dev(1 - zh, 1 - zl, x, y, c)
    partner_sibling = dev(1 - zh, 1 - zl, x, y, 1 - c)
    twin = dev(zh, 1 - zl, x, y, c)
    twin_sibling = dev(zh, 1 - zl, x, y, 1 - c)

    def near(dx, dy, dz):
        return dev(zh, (zl + dz) % 2, (x + dx) % 4, (y + dy) % 4, c)

    peers = [near(d, 0, 0) for d in (1, 2, 3)] + [near(0, d, 0) for d in (1, 2, 3)]
    peers += [partner, twin, sibling]
    barrier = pltpu.get_barrier_semaphore()
    for peer in peers:
        pl.semaphore_signal(barrier, inc=1, device_id=peer, device_id_type=MESH)

    def remote(src, dst, send, recv, device):
        return pltpu.make_async_remote_copy(
            src_ref=src, dst_ref=dst, send_sem=send, recv_sem=recv,
            device_id=device, device_id_type=MESH,
        )

    p_in = pltpu.make_async_copy(p_hbm, P_in, in_s.at[0])
    c_in = pltpu.make_async_copy(cent_hbm.at[pl.ds(pl.multiple_of(c * 128, 128), 128), :], C_in, in_s.at[1])
    p_in.start()
    c_in.start()

    def along(h, phase, step):
        if (h + phase) % 2 == 0:
            return near(step, 0, 0)
        return near(0, step, 0)

    def place(h, phase):
        return (x, y) if (h + phase) % 2 == 0 else (y, x)

    def block(h, a, b, part, parts):
        n = SUB // parts
        at = h * 1024 + b * GROUP + a * SUB + part * n
        return C.at[pl.ds(pl.multiple_of(at, n), n), :]

    def a0_copy(h, d, sent=True):
        a, b = place(h, 0)
        ref = block(h, a if sent else (a + 4 - d) % 4, b, 0, 1)
        return remote(ref, ref, a0_s.at[h, d - 1], a0_r.at[h, d - 1], along(h, 0, d))

    def a1_copy(h, j, way, k, sent=True):
        a, b = place(h, 0)
        back = (3 if way == 0 else 1)
        src = b if sent else (b + back) % 4
        if k == 2:
            src = (b + (back if sent else 2)) % 4
        half = way if k != 1 else 1 - way
        ref = block(h, (a + 4 - j) % 4, src, half, 2)
        return remote(
            ref, ref, a1_s.at[h, j, way, k], a1_r.at[h, j, way, k], along(h, 1, 1 if way == 0 else 3)
        )

    def a1_start(j, k):
        for h in (0, 1):
            for way in (0, 1):
                a1_copy(h, j, way, k).start()

    def a1_relay(j):
        for h in (0, 1):
            for way in (0, 1):
                a1_copy(h, j, way, 0, False).wait_recv()
                a1_copy(h, j, way, 2).start()

    def a1_wait(j, k):
        for h in (0, 1):
            for way in (0, 1):
                a1_copy(h, j, way, k, False).wait_recv()

    def rows(zh_, k, core):
        return pl.ds(pl.multiple_of(zh_ * 1024 + k * 256 + core * CHUNK, CHUNK), CHUNK)

    chunks = OWN // CHUNK

    def p_copy(zh_, core, k, send, recv, device):
        ref = U.at[rows(zh_, k, core), :]
        return remote(ref, ref, send.at[k], recv.at[k], device)

    def p_z(k, sent=True):
        return p_copy(zh if sent else 1 - zh, c, k, pz_s, pz_r, partner)

    def p_sib(k, sent=True):
        return p_copy(zh, c if sent else 1 - c, k, ps_s, ps_r, sibling)

    def p_fwd(k, sent=True):
        return p_copy(1 - zh, c if sent else 1 - c, k, pf_s, pf_r, sibling)

    def forward(k):
        p_z(k, False).wait_recv()
        p_fwd(k).start()

    p_in.wait()
    for k in range(chunks):
        U[rows(zh, k, c), :] = unit(P_in[pl.ds(k * CHUNK, CHUNK), :])
    c_in.wait()
    for h in (0, 1):
        a, b = place(h, 0)
        at = pl.multiple_of(h * 1024 + b * GROUP + a * SUB, SUB)
        C[pl.ds(at, SUB), :] = unit(C_in[pl.ds(h * SUB, SUB), :])

    pl.semaphore_wait(barrier, len(peers))
    p_z(0).start()
    for h in (0, 1):
        for d in (1, 3):
            a0_copy(h, d).start()
    for h in (0, 1):
        a0_copy(h, 2).start()
    a1_start(0, 0)
    for k in range(chunks):
        p_sib(k).start()
    for k in range(1, chunks):
        p_z(k).start()

    def gemm1(at, m, qt, n, first):
        s = lax.dot_general(
            C[pl.ds(at, m), :], U[pl.ds(qt, n), :],
            (((1,), (1,)), ((), ())), preferred_element_type=F32,
        )
        e = jnp.exp2(s * LOG2E20)
        K[pl.ds(at, m), pl.ds(qt, n)] = e
        Kb[pl.ds(at, m), pl.ds(qt, n)] = e.astype(BF16)
        part = [e[:, t * 128 : (t + 1) * 128] for t in range(n // 128)]
        while len(part) > 1:
            part = [part[t] + part[t + 1] for t in range(0, len(part), 2)]
        csum[pl.ds(at, m), :] = part[0] if first else csum[pl.ds(at, m), :] + part[0]

    own_rows = pl.multiple_of(zh * 1024, 1024)
    far_rows = pl.multiple_of((1 - zh) * 1024, 1024)

    def group_at(h, step):
        return pl.multiple_of(h * 1024 + (place(h, 1)[0] + step) % 4 * GROUP, GROUP)

    def own_gemm(steps):
        for step in steps:
            for h in (0, 1):
                gemm1(group_at(h, step), GROUP, own_rows, 1024, True)

    def far_gemm(k, steps):
        for step in steps:
            for h in (0, 1):
                gemm1(group_at(h, step), GROUP, pl.multiple_of(far_rows + k * 256, 256), 256, False)

    def a0_wait(d):
        for h in (0, 1):
            a0_copy(h, d, False).wait_recv()

    a0_wait(1)
    a1_start(1, 0)
    a0_wait(3)
    a1_start(3, 0)
    a1_start(0, 1)
    a0_wait(2)
    a1_start(2, 0)
    for j in (1, 3, 2):
        a1_start(j, 1)
    a1_relay(0)
    for k in range(chunks):
        p_sib(k, False).wait_recv()
    own_gemm((0,))
    forward(0)
    a1_relay(1)
    a1_relay(3)
    a1_relay(2)
    p_fwd(0, False).wait_recv()
    far_gemm(0, (0,))
    forward(1)
    for j in (0, 1, 3, 2):
        a1_wait(j, 1)
    own_gemm((1, 3))
    far_gemm(0, (1, 3))
    p_fwd(1, False).wait_recv()
    far_gemm(1, (0, 1, 3))
    forward(2)
    for j in (0, 1, 3, 2):
        a1_wait(j, 2)
    pl.semaphore_signal(ready, inc=1, device_id=twin, device_id_type=MESH)
    own_gemm((2,))
    far_gemm(0, (2,))
    far_gemm(1, (2,))
    p_fwd(2, False).wait_recv()
    far_gemm(2, (0, 1, 3, 2))
    forward(3)
    p_fwd(3, False).wait_recv()
    far_gemm(3, (0, 1, 3, 2))
    pl.semaphore_wait(ready, 1)

    def col_pass(r16):
        r = [jnp.broadcast_to(r16[t : t + 1, :], (8, 128)) for t in range(TILES)]

        @pl.loop(0, SIDE // 128)
        def _(i):
            for s in range(16):
                at = pl.multiple_of(i * 128 + s * 8, 8)
                acc = [None] * 4
                for t in range(TILES):
                    term = K[pl.ds(at, 8), t * 128 : (t + 1) * 128] * r[t]
                    acc[t % 4] = term if acc[t % 4] is None else acc[t % 4] + term
                csum[pl.ds(at, 8), :] = (acc[0] + acc[1]) + (acc[2] + acc[3])

    def fold():
        parts = []
        for b in range(TILES):
            square = csum[b * 128 : (b + 1) * 128, :]
            parts.append(jnp.sum(square.T, axis=0, keepdims=True))
        return jnp.concatenate(parts, axis=0)

    def col_send(it, value):
        colbuf[it] = value
        for k, delta in enumerate(PEERS):
            remote(colbuf.at[it], colrecv.at[it, k], col_s.at[it], col_r.at[it], near(*delta)).start()

    def col_all(it):
        return remote(colrecv.at[it], colrecv.at[it], col_s.at[it], col_r.at[it], near(*PEERS[0]))

    def col_take(it):
        col_all(it).wait_recv()
        return jnp.sum(colrecv[it], axis=0) + colbuf[it]

    def row_pass():
        def step(i, acc):
            acc = list(acc)
            for s in range(8):
                at = pl.multiple_of(i * 64 + s * 8, 8)
                scale = cb[pl.ds(at, 8), :]
                for t in range(TILES):
                    acc[t] += K[pl.ds(at, 8), t * 128 : (t + 1) * 128] * scale
            return tuple(acc)

        zero = tuple(jnp.zeros((8, 128), F32) for _ in range(TILES))
        acc = lax.fori_loop(0, SIDE // 64, step, zero)
        return jnp.concatenate([jnp.sum(a, axis=0, keepdims=True) for a in acc], axis=0)

    row_peers = (partner_sibling, partner, sibling)

    def row_copy(it, k):
        return remote(rowbuf.at[it], rowrecv.at[it, k], row_s.at[it, k], row_r.at[it, k], row_peers[k])

    def row_sum(it, value):
        rowbuf[it] = value
        for k in range(3):
            row_copy(it, k).start()
        total = value
        for k in (2, 1, 0):
            row_copy(it, k).wait_recv()
            total += rowrecv[it, k]
        return total

    r16 = None
    for it in range(ITERS):
        if it > 0:
            col_pass(r16)
        col_send(it, fold())
        c16 = TARGET / col_take(it)
        for b in range(TILES):
            cb[b * 128 : (b + 1) * 128, :] = spread(c16[b : b + 1, :])
        r16 = 1.0 / row_sum(it, row_pass())

    for b in range(TILES):
        scale = spread(r16[b : b + 1, :])
        wide = U[b * 128 : (b + 1) * 128, :].astype(F32)
        Us[b * 128 : (b + 1) * 128, :] = (
            wide * jnp.concatenate([scale] * (D // 128), axis=1)
        ).astype(BF16)

    def gemm2(h, step):
        return jnp.dot(Kb[pl.ds(group_at(h, step), GROUP), :], Us[...], preferred_element_type=F32)

    HALF = GROUP // 2

    def cols(w):
        return slice(w * WAVE, (w + 1) * WAVE)

    def rs_copy(h, w, way, k):
        lanes = pl.ds(w * WAVE, WAVE)
        if k == 0:
            src, dst = Sb.at[h, 2, pl.ds(way * HALF, HALF), lanes], Rl.at[h, way, :, lanes]
        else:
            half = 1 - way if k == 1 else way
            src, dst = (b.at[h, way, pl.ds(half * HALF, HALF), lanes] for b in (Sb, Sr))
        return remote(
            src, dst, rs_s.at[h, w, way, k], rs_r.at[h, w, way, k], along(h, 1, 1 if way == 0 else 3)
        )

    def rs_add(h, w, way):
        half = pl.ds(way * HALF, HALF)
        rs_copy(h, w, way, 0).wait_recv()
        Sb[h, way, half, cols(w)] = (Acc[h, way, :, cols(w)] + Rl[h, way, :, cols(w)].astype(F32)).astype(BF16)
        rs_copy(h, w, way, 2).start()

    for h in (0, 1):
        Sb[h, 2] = gemm2(h, 2).astype(BF16)
        for w in (0, 1):
            for way in (0, 1):
                rs_copy(h, w, way, 0).start()

    for way, step in ((0, 1), (1, 3)):
        for h in (0, 1):
            value = gemm2(h, step)
            other = 1 - way
            Sb[h, way, pl.ds(other * HALF, HALF), :] = value[other * HALF : (other + 1) * HALF, :].astype(BF16)
            Acc[h, way] = value[way * HALF : (way + 1) * HALF, :]
            for w in (0, 1):
                rs_copy(h, w, way, 1).start()
    for way in (0, 1):
        for h in (0, 1):
            rs_add(h, 0, way)
    for h in (0, 1):
        Own[h] = gemm2(h, 0)
    for way in (0, 1):
        for h in (0, 1):
            rs_add(h, 1, way)
    col_pass(r16)
    col_send(ITERS, fold())

    mass16 = col_take(ITERS)
    colbuf[ITERS + 1] = mass16
    for h in (0, 1):
        a, b = place(h, 0)
        mine = pl.ds(h * SUB, SUB)
        wt[...] = spread(colbuf[ITERS + 1, pl.ds(h * 8 + b * 2 + a // 2, 1), :])
        wbuf[mine, :] = wt[pl.ds(pl.multiple_of((a % 2) * SUB, SUB), SUB), :]
        scale = cb[pl.ds(pl.multiple_of(h * 1024 + b * GROUP + a * SUB, SUB), SUB), :]
        wt[mine, :] = wbuf[mine, :] * scale
        if h == 0:
            held = wt[mine, :]
    mass = jnp.concatenate([held, wt[pl.ds(SUB, SUB), :]], axis=0).T[0:8, :]
    mbuf[0] = mass
    mass_copy = remote(mbuf.at[0], mbuf.at[1], m_s.at[0], m_r.at[0], sibling)
    mass_copy.start()

    def r2_copy(h, w, d):
        lanes = pl.ds(w * WAVE, WAVE)
        return remote(
            Tb.at[h, d - 1, :, lanes], Tr.at[h, d - 1, :, lanes],
            r2_s.at[h, w, d - 1], r2_r.at[h, w, d - 1], along(h, 0, d),
        )

    def sub(h, d):
        return pl.ds(pl.multiple_of((place(h, 0)[0] + d) % 4 * SUB, SUB), SUB)

    for w in (0, 1):
        for h in (0, 1):
            for way in (0, 1):
                for k in (1, 2):
                    rs_copy(h, w, way, k).wait_recv()
            Own[h, :, cols(w)] += Sr[h, 0, :, cols(w)].astype(F32) + Sr[h, 1, :, cols(w)].astype(F32)
            for d in (2, 1, 3):
                Tb[h, d - 1, :, cols(w)] = Own[h, sub(h, d), cols(w)].astype(BF16)
                r2_copy(h, w, d).start()

    fin_peers = (
        (twin, (1 - zl) * 2 + c),
        (sibling, zl * 2 + 1 - c),
        (twin_sibling, (1 - zl) * 2 + 1 - c),
    )

    def fin_copy(k):
        return remote(Fs.at[fin_peers[k][1]], Fr.at[k], fin_s.at[k], fin_r.at[k], fin_peers[k][0])

    for w in (0, 1):
        for h in (0, 1):
            total = Own[h, sub(h, 0), cols(w)]
            for d in (2, 1, 3):
                r2_copy(h, w, d).wait_recv()
                total += Tr[h, d - 1, :, cols(w)].astype(F32)
            weight = 1.0 / wbuf[pl.ds(h * SUB, SUB), :]
            total *= jnp.concatenate([weight] * (WAVE // 128), axis=1)
            Own[h, sub(h, 0), cols(w)] = total
            for k in (0, 1):
                Fs[2 * w + k, pl.ds(h * SUB, SUB), :] = total[:, k * WIDTH : (k + 1) * WIDTH].astype(BF16)
    for k in (2, 0, 1):
        fin_copy(k).start()

    mass_copy.wait_recv()
    mass_ref[0:1, :] = mbuf[c, 0:1, :]
    mass_ref[1:2, :] = mbuf[1 - c, 0:1, :]

    def turned(value):
        return jnp.concatenate(
            [value[:, 0:128].T, jnp.concatenate([value[:, 128:192], jnp.zeros((128, 64), F32)], axis=1).T[0:64, :]],
            axis=0,
        )

    mine = jnp.concatenate([Own[h, sub(h, 0), :] for h in (0, 1)], axis=0)
    own_piece = mine[:, 0:WIDTH]
    for k in (1, 2, 3):
        own_piece = jnp.where(dp == k, mine[:, k * WIDTH : (k + 1) * WIDTH], own_piece)
    fin_copy(1).wait_recv()
    fin_copy(0).wait_recv()
    fin_copy(2).wait_recv()
    out_ref[:, pl.ds(pl.multiple_of(c * 128, 128), 128)] = turned(own_piece + Fr[0].astype(F32))
    out_ref[:, pl.ds(pl.multiple_of((1 - c) * 128, 128), 128)] = turned(Fr[1].astype(F32) + Fr[2].astype(F32))

    for h in (0, 1):
        for d in (1, 2, 3):
            a0_copy(h, d).wait_send()
            for w in (0, 1):
                r2_copy(h, w, d).wait_send()
        for way in (0, 1):
            for k in (0, 1, 2):
                for j in range(4):
                    a1_copy(h, j, way, k).wait_send()
                for w in (0, 1):
                    rs_copy(h, w, way, k).wait_send()
    for k in range(chunks):
        p_z(k).wait_send()
        p_sib(k).wait_send()
        p_fwd(k).wait_send()
    for it in range(ITERS + 1):
        col_all(it).wait_send()
    for it in range(ITERS):
        for k in range(3):
            row_copy(it, k).wait_send()
    mass_copy.wait_send()
    for k in range(3):
        fin_copy(k).wait_send()


def on_device(passages, centroids):
    lists = centroids.shape[0]
    chunks = OWN // CHUNK
    dma = pltpu.SemaphoreType.DMA
    vm = pltpu.VMEM
    new, mass = pl.pallas_call(
        body,
        out_shape=(
            jax.ShapeDtypeStruct((WIDTH, lists), F32),
            jax.ShapeDtypeStruct((2, 128), F32),
        ),
        in_specs=[pl.BlockSpec(memory_space=pl.ANY)] * 2,
        out_specs=(pl.BlockSpec(memory_space=pltpu.VMEM),) * 2,
        scratch_shapes=[
            vm((OWN, D), BF16),
            vm((128, D), BF16),
            vm((SIDE, D), BF16),
            vm((SIDE, D), BF16),
            vm((SIDE, D), BF16),
            vm((SIDE, SIDE), F32),
            vm((SIDE, SIDE), BF16),
            vm((SIDE, 128), F32),
            vm((SIDE, 128), F32),
            vm((ITERS + 2, TILES, 128), F32),
            vm((ITERS + 1, len(PEERS), TILES, 128), F32),
            vm((ITERS, TILES, 128), F32),
            vm((ITERS, 3, TILES, 128), F32),
            vm((2, 3, GROUP, D), BF16),
            vm((2, 2, GROUP, D), BF16),
            vm((2, 2, GROUP // 2, D), BF16),
            vm((2, 2, GROUP // 2, D), F32),
            vm((2, GROUP, D), F32),
            vm((2, 3, SUB, D), BF16),
            vm((2, 3, SUB, D), BF16),
            vm((4, 128, WIDTH), BF16),
            vm((3, 128, WIDTH), BF16),
            vm((128, 128), F32),
            vm((128, 128), F32),
            vm((2, 8, 128), F32),
            dma((2,)),
            dma((2, 3)), dma((2, 3)),
            dma((2, 4, 2, 3)), dma((2, 4, 2, 3)),
            dma((chunks,)), dma((chunks,)),
            dma((chunks,)), dma((chunks,)),
            dma((chunks,)), dma((chunks,)),
            dma((ITERS + 1,)), dma((ITERS + 1,)),
            dma((ITERS, 3)), dma((ITERS, 3)),
            dma((2, 2, 2, 3)), dma((2, 2, 2, 3)),
            dma((2, 2, 3)), dma((2, 2, 3)),
            dma((3,)), dma((3,)),
            dma((1,)), dma((1,)),
            pltpu.SemaphoreType.REGULAR,
        ],
        compiler_params=pltpu.CompilerParams(
            collective_id=0, has_side_effects=True, vmem_limit_bytes=60 * 1024 * 1024
        ),
        cost_estimate=pl.CostEstimate(
            flops=4 * SIDE * SIDE * D, bytes_accessed=2 * 1024 * 1024, transcendentals=SIDE * SIDE
        ),
        name="sinkhorn",
    )(passages, centroids)
    return new.T, mass.reshape(lists)


def solution(mesh):
    return jax.shard_map(
        on_device,
        mesh=mesh,
        in_specs=(P(("dp", "list"), None), P("list", None)),
        out_specs=(P("list", "dp"), P("list")),
        check_vma=False,
    )
```

```python
import jax
import jax.numpy as jnp
from jax import lax
from jax.experimental import pallas as pl
from jax.experimental.pallas import tpu as pltpu
from jax.sharding import PartitionSpec as P

MESH = pl.DeviceIdType.MESH
F32 = jnp.float32
BF16 = jnp.bfloat16

ITERS = 3
D = 768
LISTS = 1024
ROWS = 4096
OWN = 512
CHUNK = 128
GROUP = 128
SUB = 32
HALFLISTS = LISTS // 2
MINE = 2 * SUB
LT = LISTS // 128
RT = ROWS // 128
TARGET = 8.0
LOG2E20 = 20.0 * 1.4426950408889634

WIDTH = D // 4
WAVE = D // 2


def far_first():
    deltas = [(a, b) for a in range(4) for b in range(4) if (a, b) != (0, 0)]
    return tuple(sorted(deltas, key=lambda d: -(min(d[0], 4 - d[0]) + min(d[1], 4 - d[1]))))


PEERS = far_first()


def unit(values):
    wide = values.astype(F32)
    return (wide * lax.rsqrt(jnp.sum(wide * wide, axis=-1, keepdims=True) + 1e-06)).astype(BF16)


def spread(row):
    return jnp.broadcast_to(row, (128, 128)).T


def body(
    p_hbm, cent_hbm, out_ref, mass_ref,
    P_in, C_in, U, Us, C, K, Kb, csum, cb, colbuf, colrecv, rowbuf, rowrecv,
    Sb, Sr, Rl, Acc, Own, Tb, Tr, Fs, Fr, wt, wbuf, mbuf,
    in_s, a0_s, a0_r, a1_s, a1_r, ps_s, ps_r, pz_s, pz_r, pr_s, pr_r, pf_s, pf_r, col_s, col_r, row_s, row_r,
    rs_s, rs_r, r2_s, r2_r, fin_s, fin_r, m_s, m_r,
):
    dp = lax.axis_index("dp")
    li = lax.axis_index("list")
    zl, c = dp // 2, dp % 2
    zh, x, y = li // 16, (li // 4) % 4, li % 4

    def dev(zh_, zl_, x_, y_, c_):
        return (zl_ * 2 + c_, zh_ * 16 + x_ * 4 + y_)

    z = zh * 2 + zl
    sibling = dev(zh, zl, x, y, 1 - c)

    def up(d, core):
        to = (z + d) % 4
        return dev(to // 2, to % 2, x, y, core)

    def near(dx, dy):
        return dev(zh, zl, (x + dx) % 4, (y + dy) % 4, c)

    peers = [near(d, 0) for d in (1, 2, 3)] + [near(0, d) for d in (1, 2, 3)]
    peers += [up(1, c), up(3, c), sibling]
    barrier = pltpu.get_barrier_semaphore()
    for peer in peers:
        pl.semaphore_signal(barrier, inc=1, device_id=peer, device_id_type=MESH)

    def remote(src, dst, send, recv, device):
        return pltpu.make_async_remote_copy(
            src_ref=src, dst_ref=dst, send_sem=send, recv_sem=recv,
            device_id=device, device_id_type=MESH,
        )

    p_in = pltpu.make_async_copy(p_hbm, P_in, in_s.at[0])
    c_in = pltpu.make_async_copy(cent_hbm.at[pl.ds(pl.multiple_of(dp * MINE, MINE), MINE), :], C_in, in_s.at[1])
    p_in.start()
    c_in.start()

    def along(h, phase, step):
        if (h + phase) % 2 == 0:
            return near(step, 0)
        return near(0, step)

    def place(h, phase):
        return (x, y) if (h + phase) % 2 == 0 else (y, x)

    def block(h, a, b, part, parts):
        n = SUB // parts
        at = h * HALFLISTS + b * GROUP + a * SUB + part * n
        return C.at[pl.ds(pl.multiple_of(at, n), n), :]

    def a0_copy(h, d, sent=True):
        a, b = place(h, 0)
        ref = block(h, a if sent else (a + 4 - d) % 4, b, 0, 1)
        return remote(ref, ref, a0_s.at[h, d - 1], a0_r.at[h, d - 1], along(h, 0, d))

    def a1_copy(h, j, way, k, sent=True):
        a, b = place(h, 0)
        back = (3 if way == 0 else 1)
        src = b if sent else (b + back) % 4
        if k == 2:
            src = (b + (back if sent else 2)) % 4
        half = way if k != 1 else 1 - way
        ref = block(h, (a + 4 - j) % 4, src, half, 2)
        return remote(
            ref, ref, a1_s.at[h, j, way, k], a1_r.at[h, j, way, k], along(h, 1, 1 if way == 0 else 3)
        )

    def a1_start(j, k):
        for h in (0, 1):
            for way in (0, 1):
                a1_copy(h, j, way, k).start()

    def a1_relay(j):
        for h in (0, 1):
            for way in (0, 1):
                a1_copy(h, j, way, 0, False).wait_recv()
                a1_copy(h, j, way, 2).start()

    def a1_wait(j, k):
        for h in (0, 1):
            for way in (0, 1):
                a1_copy(h, j, way, k, False).wait_recv()

    def rows(at, k, core):
        return pl.ds(pl.multiple_of(at * 1024 + k * 256 + core * CHUNK, CHUNK), CHUNK)

    chunks = OWN // CHUNK

    def p_copy(d, core, k, send, recv, device):
        ref = U.at[rows((z + d) % 4, k, core), :]
        return remote(ref, ref, send, recv, device)

    def p_sib(k, sent=True):
        return p_copy(0, c if sent else 1 - c, k, ps_s.at[k], ps_r.at[k], sibling)

    def p_z(k, way, sent=True):
        step = 1 if way == 0 else 3
        return p_copy(0 if sent else 4 - step, c, k, pz_s.at[way, k], pz_r.at[way, k], up(step, c))

    def p_relay(k, sent=True):
        step = 1 if k < 2 else 3
        return p_copy(4 - step if sent else 2, c, k, pr_s.at[k], pr_r.at[k], up(step, c))

    def p_fwd(d, k, sent=True):
        return p_copy(d, c if sent else 1 - c, k, pf_s.at[d - 1, k], pf_r.at[d - 1, k], sibling)

    def p_near(k):
        for way in (0, 1):
            p_z(k, way, False).wait_recv()
            if (k < 2) == (way == 0):
                p_relay(k).start()
        for d in (1, 3):
            p_fwd(d, k).start()

    def p_far(k):
        p_relay(k, False).wait_recv()
        p_fwd(2, k).start()

    p_in.wait()
    for k in range(chunks):
        U[rows(z, k, c), :] = unit(P_in[pl.ds(k * CHUNK, CHUNK), :])
    c_in.wait()
    for h in (0, 1):
        a, b = place(h, 0)
        at = pl.multiple_of(h * HALFLISTS + b * GROUP + a * SUB, SUB)
        C[pl.ds(at, SUB), :] = unit(C_in[pl.ds(h * SUB, SUB), :])

    pl.semaphore_wait(barrier, len(peers))
    for k in (0, 2):
        for way in (0, 1):
            p_z(k, way).start()
    for h in (0, 1):
        for d in (1, 3):
            a0_copy(h, d).start()
    for h in (0, 1):
        a0_copy(h, 2).start()
    a1_start(0, 0)
    for k in range(chunks):
        p_sib(k).start()
    for k in (1, 3):
        for way in (0, 1):
            p_z(k, way).start()

    def gemm1(at, m, qt, n, first):
        s = lax.dot_general(
            C[pl.ds(at, m), :], U[pl.ds(qt, n), :],
            (((1,), (1,)), ((), ())), preferred_element_type=F32,
        )
        e = jnp.exp2(s * LOG2E20)
        K[pl.ds(at, m), pl.ds(qt, n)] = e
        Kb[pl.ds(at, m), pl.ds(qt, n)] = e.astype(BF16)
        part = [e[:, t * 128 : (t + 1) * 128] for t in range(n // 128)]
        while len(part) > 1:
            part = [part[t] + part[t + 1] for t in range(0, len(part), 2)]
        csum[pl.ds(at, m), :] = part[0] if first else csum[pl.ds(at, m), :] + part[0]

    def group_at(h, step):
        return pl.multiple_of(h * HALFLISTS + (place(h, 1)[0] + step) % 4 * GROUP, GROUP)

    def own_gemm(steps):
        for step in steps:
            for h in (0, 1):
                gemm1(group_at(h, step), GROUP, pl.multiple_of(z * 1024, 1024), 1024, True)

    def far_gemm(d, k):
        at = pl.multiple_of((z + d) % 4 * 1024 + k * 256, 256)
        for g in range(0, LISTS, 256):
            gemm1(g, 256, at, 256, False)

    def a0_wait(d):
        for h in (0, 1):
            a0_copy(h, d, False).wait_recv()

    a0_wait(1)
    a1_start(1, 0)
    a0_wait(3)
    a1_start(3, 0)
    a1_start(0, 1)
    a0_wait(2)
    a1_start(2, 0)
    for j in (1, 3, 2):
        a1_start(j, 1)
    a1_relay(0)
    for k in range(chunks):
        p_sib(k, False).wait_recv()
    own_gemm((0,))
    a1_relay(1)
    a1_relay(3)
    p_near(0)
    a1_relay(2)
    for j in (0, 1, 3, 2):
        a1_wait(j, 1)
    own_gemm((1, 3))
    p_near(2)
    for j in (0, 1, 3, 2):
        a1_wait(j, 2)
    own_gemm((2,))
    p_near(1)

    def far_both(k):
        for d in (1, 3):
            p_fwd(d, k, False).wait_recv()
        for d in (1, 3):
            far_gemm(d, k)

    def far_two(k):
        p_fwd(2, k, False).wait_recv()
        far_gemm(2, k)

    far_both(0)
    p_far(0)
    far_both(2)
    p_near(3)
    p_far(2)
    far_both(1)
    far_two(0)
    p_far(1)
    far_two(2)
    far_both(3)
    p_far(3)
    far_two(1)
    far_two(3)

    def col_pass(r16, out):
        strips = 32

        @pl.loop(0, LISTS // (8 * strips))
        def _(i):
            acc = [None] * strips
            for t in range(RT):
                r = jnp.broadcast_to(r16[t : t + 1, :], (8, 128))
                for s in range(strips):
                    at = pl.multiple_of(i * (8 * strips) + s * 8, 8)
                    term = K[pl.ds(at, 8), t * 128 : (t + 1) * 128] * r
                    acc[s] = term if acc[s] is None else acc[s] + term
            for s in range(strips):
                csum[pl.ds(pl.multiple_of(i * (8 * strips) + s * 8, 8), 8), :] = acc[s]

        fold(out)

    def fold(out):
        parts = []
        for b in range(LT):
            square = csum[b * 128 : (b + 1) * 128, :]
            parts.append(jnp.sum(square.T, axis=0, keepdims=True))
        out[...] = jnp.concatenate(parts, axis=0)

    def col_send(it):
        for k, delta in enumerate(PEERS):
            remote(colbuf.at[it], colrecv.at[it, k], col_s.at[it], col_r.at[it], near(*delta)).start()

    def col_all(it):
        return remote(colrecv.at[it], colrecv.at[it], col_s.at[it], col_r.at[it], near(*PEERS[0]))

    def col_take(it):
        col_all(it).wait_recv()
        return jnp.sum(colrecv[it], axis=0) + colbuf[it]

    def row_pass(c16):
        for b in range(LT):
            cb[b * 128 : (b + 1) * 128, :] = spread(c16[b : b + 1, :])

        def step(i, acc):
            acc = list(acc)
            for s in range(8):
                at = pl.multiple_of(i * 64 + s * 8, 8)
                scale = cb[pl.ds(at, 8), :]
                for t in range(RT):
                    acc[t] += K[pl.ds(at, 8), t * 128 : (t + 1) * 128] * scale
            return tuple(acc)

        zero = tuple(jnp.zeros((8, 128), F32) for _ in range(RT))
        acc = lax.fori_loop(0, LISTS // 64, step, zero)
        return jnp.concatenate([jnp.sum(a, axis=0, keepdims=True) for a in acc], axis=0)

    row_peers = [up(2, 1 - c), up(2, c)] + [up(d, 1 - c) for d in (1, 3)] + [up(d, c) for d in (1, 3)] + [sibling]

    def row_send(it, value):
        rowbuf[it] = value
        for k, peer in enumerate(row_peers):
            remote(rowbuf.at[it], rowrecv.at[it, k], row_s.at[it], row_r.at[it], peer).start()

    def row_all(it):
        return remote(rowrecv.at[it], rowrecv.at[it], row_s.at[it], row_r.at[it], sibling)

    def row_sum(it, value):
        row_send(it, value)
        row_all(it).wait_recv()
        return jnp.sum(rowrecv[it], axis=0) + value

    r16 = None
    for it in range(ITERS):
        if it == 0:
            fold(colbuf.at[0])
        else:
            col_pass(r16, colbuf.at[it])
        col_send(it)
        r16 = 1.0 / row_sum(it, row_pass(TARGET / col_take(it)))

    def scale_rows(first, count):
        for b in range(first, first + count):
            scale = spread(r16[b : b + 1, :])
            wide = U[b * 128 : (b + 1) * 128, :].astype(F32)
            Us[b * 128 : (b + 1) * 128, :] = (
                wide * jnp.concatenate([scale] * (D // 128), axis=1)
            ).astype(BF16)

    def gemm2(h, step):
        return jnp.dot(Kb[pl.ds(group_at(h, step), GROUP), :], Us[...], preferred_element_type=F32)

    def gemm2_first(h, step, parts=8):
        total = None
        n = ROWS // parts
        for q in range(parts):
            scale_rows(q * (RT // parts), RT // parts)
            part = jnp.dot(
                Kb[pl.ds(group_at(h, step), GROUP), q * n : (q + 1) * n], Us[q * n : (q + 1) * n, :],
                preferred_element_type=F32,
            )
            total = part if total is None else total + part
        return total

    HALF = GROUP // 2

    def cols(w):
        return slice(w * WAVE, (w + 1) * WAVE)

    def rs_copy(h, w, way, k):
        lanes = pl.ds(w * WAVE, WAVE)
        if k == 0:
            src, dst = Sb.at[h, 2, pl.ds(way * HALF, HALF), lanes], Rl.at[h, way, :, lanes]
        else:
            half = 1 - way if k == 1 else way
            src, dst = (b.at[h, way, pl.ds(half * HALF, HALF), lanes] for b in (Sb, Sr))
        return remote(
            src, dst, rs_s.at[h, w, way, k], rs_r.at[h, w, way, k], along(h, 1, 1 if way == 0 else 3)
        )

    def rs_add(h, w, way):
        half = pl.ds(way * HALF, HALF)
        rs_copy(h, w, way, 0).wait_recv()
        Sb[h, way, half, cols(w)] = (Acc[h, way, :, cols(w)] + Rl[h, way, :, cols(w)].astype(F32)).astype(BF16)
        rs_copy(h, w, way, 2).start()

    for h in (0, 1):
        Sb[h, 2] = (gemm2_first if h == 0 else gemm2)(h, 2).astype(BF16)
        for w in (0, 1):
            for way in (0, 1):
                rs_copy(h, w, way, 0).start()

    for way, step in ((0, 1), (1, 3)):
        for h in (0, 1):
            value = gemm2(h, step)
            other = 1 - way
            Sb[h, way, pl.ds(other * HALF, HALF), :] = value[other * HALF : (other + 1) * HALF, :].astype(BF16)
            Acc[h, way] = value[way * HALF : (way + 1) * HALF, :]
            rs_copy(h, 0, way, 1).start()
    for way in (0, 1):
        for h in (0, 1):
            rs_add(h, 0, way)
            rs_copy(h, 1, way, 1).start()
    for h in (0, 1):
        Own[h] = gemm2(h, 0)
    for way in (0, 1):
        for h in (0, 1):
            rs_add(h, 1, way)
    col_pass(r16, colbuf.at[ITERS])
    col_send(ITERS)

    colbuf[ITERS + 1] = col_take(ITERS)
    held = []
    for h in (0, 1):
        a, b = place(h, 0)
        wt[...] = spread(colbuf[ITERS + 1, pl.ds(h * 4 + b, 1), :])
        wbuf[pl.ds(h * SUB, SUB), :] = wt[pl.ds(pl.multiple_of(a * SUB, SUB), SUB), :]
        scale = cb[pl.ds(pl.multiple_of(h * HALFLISTS + b * GROUP + a * SUB, SUB), SUB), :]
        held.append(wbuf[pl.ds(h * SUB, SUB), :] * scale)
    mass = jnp.concatenate(held + [jnp.zeros((128 - MINE, 128), F32)], axis=0).T[0:8, :]
    mbuf[dp] = mass
    fin_peers = (
        (dev(zh, 1 - zl, x, y, 1 - c), (1 - zl) * 2 + 1 - c),
        (dev(zh, 1 - zl, x, y, c), (1 - zl) * 2 + c),
        (sibling, zl * 2 + 1 - c),
    )

    def mass_copy(k, sent=True):
        slot = mbuf.at[dp if sent else fin_peers[k][1]]
        return remote(slot, slot, m_s.at[k], m_r.at[k], fin_peers[k][0])

    for k in range(3):
        mass_copy(k).start()

    def r2_copy(h, w, d):
        lanes = pl.ds(w * WAVE, WAVE)
        return remote(
            Tb.at[h, d - 1, :, lanes], Tr.at[h, d - 1, :, lanes],
            r2_s.at[h, w, d - 1], r2_r.at[h, w, d - 1], along(h, 0, d),
        )

    def sub(h, d):
        return pl.ds(pl.multiple_of((place(h, 0)[0] + d) % 4 * SUB, SUB), SUB)

    for w in (0, 1):
        for h in (0, 1):
            for way in (0, 1):
                for k in (1, 2):
                    rs_copy(h, w, way, k).wait_recv()
            Own[h, :, cols(w)] += Sr[h, 0, :, cols(w)].astype(F32) + Sr[h, 1, :, cols(w)].astype(F32)
            for d in (2, 1, 3):
                Tb[h, d - 1, :, cols(w)] = Own[h, sub(h, d), cols(w)].astype(BF16)
                r2_copy(h, w, d).start()

    def fin_copy(k, sent=True):
        to = fin_peers[k][1]
        return remote(Fs.at[to if sent else dp], Fr.at[dp if sent else to], fin_s.at[k], fin_r.at[k], fin_peers[k][0])

    for w in (0, 1):
        for h in (0, 1):
            total = Own[h, sub(h, 0), cols(w)]
            for d in (2, 1, 3):
                r2_copy(h, w, d).wait_recv()
                total += Tr[h, d - 1, :, cols(w)].astype(F32)
            weight = 1.0 / wbuf[pl.ds(h * SUB, SUB), :]
            total *= jnp.concatenate([weight] * (WAVE // 128), axis=1)
            for k in (0, 1):
                Fs[2 * w + k, pl.ds(h * SUB, SUB), :] = total[:, k * WIDTH : (k + 1) * WIDTH].astype(Fs.dtype)
    for k in range(3):
        fin_copy(k).start()

    for k in range(3):
        mass_copy(k, False).wait_recv()
    for k in (0, 1):
        mass_ref[k : k + 1, :] = jnp.concatenate([mbuf[2 * k, 0:1, 0:MINE], mbuf[2 * k + 1, 0:1, 0:MINE]], axis=1)

    Fr[dp] = Fs[dp]
    for k in (2, 1, 0):
        fin_copy(k, False).wait_recv()
    for k in (0, 1):
        value = jnp.concatenate([Fr[2 * k], Fr[2 * k + 1]], axis=0).astype(F32)
        out_ref[0:128, k * 128 : (k + 1) * 128] = value[:, 0:128].T
        side = jnp.concatenate([value[:, 128:192], jnp.zeros((128, 64), F32)], axis=1)
        out_ref[128:192, k * 128 : (k + 1) * 128] = side.T[0:64, :]

    for h in (0, 1):
        for d in (1, 2, 3):
            a0_copy(h, d).wait_send()
            for w in (0, 1):
                r2_copy(h, w, d).wait_send()
        for way in (0, 1):
            for k in (0, 1, 2):
                for j in range(4):
                    a1_copy(h, j, way, k).wait_send()
                for w in (0, 1):
                    rs_copy(h, w, way, k).wait_send()
    for k in range(chunks):
        for way in (0, 1):
            p_z(k, way).wait_send()
        p_sib(k).wait_send()
        p_relay(k).wait_send()
        for d in (1, 2, 3):
            p_fwd(d, k).wait_send()
    for it in range(ITERS + 1):
        col_all(it).wait_send()
    for it in range(ITERS):
        row_all(it).wait_send()
    for k in range(3):
        mass_copy(k).wait_send()
        fin_copy(k).wait_send()


def on_device(passages, centroids):
    lists = centroids.shape[0]
    chunks = OWN // CHUNK
    dma = pltpu.SemaphoreType.DMA
    vm = pltpu.VMEM
    new, mass = pl.pallas_call(
        body,
        out_shape=(
            jax.ShapeDtypeStruct((WIDTH, lists), F32),
            jax.ShapeDtypeStruct((2, 128), F32),
        ),
        in_specs=[pl.BlockSpec(memory_space=pl.ANY)] * 2,
        out_specs=(pl.BlockSpec(memory_space=pltpu.VMEM),) * 2,
        scratch_shapes=[
            vm((OWN, D), BF16),
            vm((MINE, D), BF16),
            vm((ROWS, D), BF16),
            vm((ROWS, D), BF16),
            vm((LISTS, D), BF16),
            vm((LISTS, ROWS), F32),
            vm((LISTS, ROWS), BF16),
            vm((LISTS, 128), F32),
            vm((LISTS, 128), F32),
            vm((ITERS + 2, LT, 128), F32),
            vm((ITERS + 1, len(PEERS), LT, 128), F32),
            vm((ITERS, RT, 128), F32),
            vm((ITERS, 7, RT, 128), F32),
            vm((2, 3, GROUP, D), BF16),
            vm((2, 2, GROUP, D), BF16),
            vm((2, 2, GROUP // 2, D), BF16),
            vm((2, 2, GROUP // 2, D), F32),
            vm((2, GROUP, D), F32),
            vm((2, 3, SUB, D), BF16),
            vm((2, 3, SUB, D), BF16),
            vm((4, MINE, WIDTH), BF16),
            vm((4, MINE, WIDTH), BF16),
            vm((128, 128), F32),
            vm((MINE, 128), F32),
            vm((4, 8, 128), F32),
            dma((2,)),
            dma((2, 3)), dma((2, 3)),
            dma((2, 4, 2, 3)), dma((2, 4, 2, 3)),
            dma((chunks,)), dma((chunks,)),
            dma((2, chunks)), dma((2, chunks)),
            dma((chunks,)), dma((chunks,)),
            dma((3, chunks)), dma((3, chunks)),
            dma((ITERS + 1,)), dma((ITERS + 1,)),
            dma((ITERS,)), dma((ITERS,)),
            dma((2, 2, 2, 3)), dma((2, 2, 2, 3)),
            dma((2, 2, 3)), dma((2, 2, 3)),
            dma((3,)), dma((3,)),
            dma((3,)), dma((3,)),
        ],
        compiler_params=pltpu.CompilerParams(
            collective_id=0, has_side_effects=True, vmem_limit_bytes=60 * 1024 * 1024
        ),
        cost_estimate=pl.CostEstimate(
            flops=4 * LISTS * ROWS * D, bytes_accessed=2 * 1024 * 1024, transcendentals=LISTS * ROWS
        ),
        name="sinkhorn",
    )(passages, centroids)
    return new.T, mass.reshape(lists)


def solution(mesh):
    return jax.shard_map(
        on_device,
        mesh=mesh,
        in_specs=(P(("dp", "list"), None), P("list", None)),
        out_specs=(P("list", "dp"), P("list")),
        check_vma=False,
    )
```

```python
import jax
import jax.numpy as jnp
from jax import lax
from jax.experimental import pallas as pl
from jax.experimental.pallas import tpu as pltpu
from jax.sharding import PartitionSpec as P

MESH = pl.DeviceIdType.MESH
F32 = jnp.float32
BF16 = jnp.bfloat16

ITERS = 3
D = 768
LISTS = 1024
ROWS = 4096
OWN = 512
CHUNK = 128
GROUP = 128
SUB = 32
HALFLISTS = LISTS // 2
MINE = 2 * SUB
LT = LISTS // 128
RT = ROWS // 128
HT = RT // 2
TARGET = 8.0
LOG2E20 = 20.0 * 1.4426950408889634

WIDTH = D // 4
WAVE = D // 2


def far_first():
    deltas = [(a, b) for a in range(4) for b in range(4) if (a, b) != (0, 0)]
    return tuple(sorted(deltas, key=lambda d: -(min(d[0], 4 - d[0]) + min(d[1], 4 - d[1]))))


PEERS = far_first()


def unit(values):
    wide = values.astype(F32)
    return (wide * lax.rsqrt(jnp.sum(wide * wide, axis=-1, keepdims=True) + 1e-06)).astype(BF16)


def spread(row):
    return jnp.broadcast_to(row, (128, 128)).T


def body(
    p_hbm, cent_hbm, out_hbm, mass_hbm,
    out_ref, mass_ref,
    P_in, C_in, U, C, K, csum, cb, colbuf, colrecv, rowbuf, rowrecv,
    Sb, Sr, Rl, Acc, Own, Tb, Tr, Fs, Fr, wt, wbuf, mbuf,
    in_s, out_s, a0_s, a0_r, a1_s, a1_r, ps_s, ps_r, pz_s, pz_r, pr_s, pr_r, pf_s, pf_r, col_s, col_r, row_s, row_r,
    rs_s, rs_r, r2_s, r2_r, fin_s, fin_r, m_s, m_r,
):
    dp = lax.axis_index("dp")
    li = lax.axis_index("list")
    zl, c = dp // 2, dp % 2
    zh, x, y = li // 16, (li // 4) % 4, li % 4

    def dev(zh_, zl_, x_, y_, c_):
        return (zl_ * 2 + c_, zh_ * 16 + x_ * 4 + y_)

    z = zh * 2 + zl
    sibling = dev(zh, zl, x, y, 1 - c)

    def up(d, core):
        to = (z + d) % 4
        return dev(to // 2, to % 2, x, y, core)

    def near(dx, dy):
        return dev(zh, zl, (x + dx) % 4, (y + dy) % 4, c)

    peers = [near(d, 0) for d in (1, 2, 3)] + [near(0, d) for d in (1, 2, 3)]
    peers += [up(1, c), up(3, c), sibling]
    barrier = pltpu.get_barrier_semaphore()
    for peer in peers:
        pl.semaphore_signal(barrier, inc=1, device_id=peer, device_id_type=MESH)

    def remote(src, dst, send, recv, device):
        return pltpu.make_async_remote_copy(
            src_ref=src, dst_ref=dst, send_sem=send, recv_sem=recv,
            device_id=device, device_id_type=MESH,
        )

    p_in = pltpu.make_async_copy(p_hbm, P_in, in_s.at[0])
    c_in = pltpu.make_async_copy(cent_hbm.at[pl.ds(pl.multiple_of(dp * MINE, MINE), MINE), :], C_in, in_s.at[1])
    p_in.start()
    c_in.start()

    def along(h, phase, step):
        if (h + phase) % 2 == 0:
            return near(step, 0)
        return near(0, step)

    def place(h, phase):
        return (x, y) if (h + phase) % 2 == 0 else (y, x)

    def block(h, a, b, part, parts):
        n = SUB // parts
        at = h * HALFLISTS + b * GROUP + a * SUB + part * n
        return C.at[pl.ds(pl.multiple_of(at, n), n), :]

    def a0_copy(h, d, sent=True):
        a, b = place(h, 0)
        ref = block(h, a if sent else (a + 4 - d) % 4, b, 0, 1)
        return remote(ref, ref, a0_s.at[h, d - 1], a0_r.at[h, d - 1], along(h, 0, d))

    def a1_copy(h, j, way, k, sent=True):
        a, b = place(h, 0)
        back = (3 if way == 0 else 1)
        src = b if sent else (b + back) % 4
        if k == 2:
            src = (b + (back if sent else 2)) % 4
        half = way if k != 1 else 1 - way
        ref = block(h, (a + 4 - j) % 4, src, half, 2)
        return remote(
            ref, ref, a1_s.at[h, j, way, k], a1_r.at[h, j, way, k], along(h, 1, 1 if way == 0 else 3)
        )

    def a1_start(j, k):
        for h in (0, 1):
            for way in (0, 1):
                a1_copy(h, j, way, k).start()

    def a1_relay(j):
        for h in (0, 1):
            for way in (0, 1):
                a1_copy(h, j, way, 0, False).wait_recv()
                a1_copy(h, j, way, 2).start()

    def a1_wait(j, k):
        for h in (0, 1):
            for way in (0, 1):
                a1_copy(h, j, way, k, False).wait_recv()

    def rows(at, k, core):
        return pl.ds(pl.multiple_of(at * 1024 + k * 256 + core * CHUNK, CHUNK), CHUNK)

    chunks = OWN // CHUNK

    def p_copy(d, core, k, send, recv, device):
        ref = U.at[rows((z + d) % 4, k, core), :]
        return remote(ref, ref, send, recv, device)

    def p_sib(k, sent=True):
        return p_copy(0, c if sent else 1 - c, k, ps_s.at[k], ps_r.at[k], sibling)

    def p_z(k, way, sent=True):
        step = 1 if way == 0 else 3
        return p_copy(0 if sent else 4 - step, c, k, pz_s.at[way, k], pz_r.at[way, k], up(step, c))

    def p_relay(k, sent=True):
        step = 1 if k < 2 else 3
        return p_copy(4 - step if sent else 2, c, k, pr_s.at[k], pr_r.at[k], up(step, c))

    def p_fwd(d, k, sent=True):
        return p_copy(d, c if sent else 1 - c, k, pf_s.at[d - 1, k], pf_r.at[d - 1, k], sibling)

    def p_near(way, k):
        p_z(k, way, False).wait_recv()
        if (k < 2) == (way == 0):
            p_relay(k).start()
        p_fwd(3 if way == 0 else 1, k).start()

    def p_far(k):
        p_relay(k, False).wait_recv()
        p_fwd(2, k).start()

    p_in.wait()
    for k in range(chunks):
        U[rows(z, k, c), :] = unit(P_in[pl.ds(k * CHUNK, CHUNK), :])
    c_in.wait()
    for h in (0, 1):
        a, b = place(h, 0)
        at = pl.multiple_of(h * HALFLISTS + b * GROUP + a * SUB, SUB)
        C[pl.ds(at, SUB), :] = unit(C_in[pl.ds(h * SUB, SUB), :])

    pl.semaphore_wait(barrier, len(peers))
    for way in (0, 1):
        p_z(2 * way, way).start()
    for h in (0, 1):
        for d in (1, 3):
            a0_copy(h, d).start()
    for h in (0, 1):
        a0_copy(h, 2).start()
    a1_start(0, 0)
    for k in range(chunks):
        p_sib(k).start()
    for k in (1, 2, 3):
        for way in (0, 1):
            p_z((k + 2 * way) % 4, way).start()

    def gemm1(at, m, qt, n, first):
        s = lax.dot_general(
            C[pl.ds(at, m), :], U[pl.ds(qt, n), :],
            (((1,), (1,)), ((), ())), preferred_element_type=F32,
        )
        e = jnp.exp2(s * LOG2E20)
        K[pl.ds(at, m), pl.ds(qt, n)] = e
        part = [e[:, t * 128 : (t + 1) * 128] for t in range(n // 128)]
        while len(part) > 1:
            part = [part[t] + part[t + 1] for t in range(0, len(part), 2)]
        csum[pl.ds(at, m), :] = part[0] if first else csum[pl.ds(at, m), :] + part[0]

    def group_at(h, step):
        return pl.multiple_of(h * HALFLISTS + (place(h, 1)[0] + step) % 4 * GROUP, GROUP)

    def own_gemm():
        for g in range(0, LISTS, 256):
            gemm1(g, 256, pl.multiple_of(z * 1024, 1024), 1024, True)

    def far_gemm(d, k):
        at = pl.multiple_of((z + d) % 4 * 1024 + k * 256, 256)
        for g in range(0, LISTS, 256):
            gemm1(g, 256, at, 256, False)

    def a0_wait(d):
        for h in (0, 1):
            a0_copy(h, d, False).wait_recv()

    a0_wait(1)
    a1_start(1, 0)
    a0_wait(3)
    a1_start(3, 0)
    a1_start(0, 1)
    a0_wait(2)
    a1_start(2, 0)
    for j in (1, 3, 2):
        a1_start(j, 1)
    a1_relay(0)
    for k in range(chunks):
        p_sib(k, False).wait_recv()
    p_near(0, 0)
    p_near(1, 2)
    a1_relay(1)
    a1_relay(3)
    a1_relay(2)
    p_near(0, 1)
    p_near(1, 3)
    for k in (1, 2):
        for j in (0, 1, 3, 2):
            a1_wait(j, k)
    own_gemm()

    def far(d, k):
        p_fwd(d, k, False).wait_recv()
        far_gemm(d, k)

    p_near(0, 2)
    p_near(1, 0)
    far(3, 0)
    far(1, 2)
    far(3, 1)
    far(1, 3)
    p_near(0, 3)
    p_near(1, 1)
    far(3, 2)
    far(1, 0)
    p_far(0)
    p_far(2)
    far(3, 3)
    far(1, 1)
    far(2, 0)
    far(2, 2)
    p_far(1)
    p_far(3)
    far(2, 1)
    far(2, 3)

    def col_pass(half, r16):
        strips = 32

        @pl.loop(0, LISTS // (8 * strips))
        def _(i):
            acc = [None] * strips
            for t in range(HT):
                r = jnp.broadcast_to(r16[t : t + 1, :], (8, 128))
                lanes = slice((half * HT + t) * 128, (half * HT + t + 1) * 128)
                for s in range(strips):
                    at = pl.multiple_of(i * (8 * strips) + s * 8, 8)
                    term = K[pl.ds(at, 8), lanes] * r
                    if t == 0 and half == 1:
                        term += csum[pl.ds(at, 8), :]
                    acc[s] = term if acc[s] is None else acc[s] + term
            for s in range(strips):
                csum[pl.ds(pl.multiple_of(i * (8 * strips) + s * 8, 8), 8), :] = acc[s]

    def fold(out):
        parts = []
        for b in range(LT):
            square = csum[b * 128 : (b + 1) * 128, :]
            parts.append(jnp.sum(square.T, axis=0, keepdims=True))
        out[...] = jnp.concatenate(parts, axis=0)

    def col_send(it):
        for k, delta in enumerate(PEERS):
            remote(colbuf.at[it], colrecv.at[it, k], col_s.at[it], col_r.at[it], near(*delta)).start()

    def col_all(it):
        return remote(colrecv.at[it], colrecv.at[it], col_s.at[it], col_r.at[it], near(*PEERS[0]))

    def col_take(it):
        col_all(it).wait_recv()
        return jnp.sum(colrecv[it], axis=0) + colbuf[it]

    def row_pass(half):
        def step(i, acc):
            acc = list(acc)
            for s in range(8):
                at = pl.multiple_of(i * 64 + s * 8, 8)
                scale = cb[pl.ds(at, 8), :]
                for t in range(HT):
                    acc[t] += K[pl.ds(at, 8), (half * HT + t) * 128 : (half * HT + t + 1) * 128] * scale
            return tuple(acc)

        zero = tuple(jnp.zeros((8, 128), F32) for _ in range(HT))
        acc = lax.fori_loop(0, LISTS // 64, step, zero)
        return jnp.concatenate([jnp.sum(a, axis=0, keepdims=True) for a in acc], axis=0)

    row_peers = [up(2, 1 - c), up(2, c)] + [up(d, 1 - c) for d in (1, 3)] + [up(d, c) for d in (1, 3)] + [sibling]

    def row_send(it, half, value):
        rowbuf[it, half] = value
        for k, peer in enumerate(row_peers):
            remote(
                rowbuf.at[it, half], rowrecv.at[it, half, k], row_s.at[it, half], row_r.at[it, half], peer
            ).start()

    def row_all(it, half):
        got = rowrecv.at[it, half]
        return remote(got, got, row_s.at[it, half], row_r.at[it, half], sibling)

    def row_take(it, half):
        row_all(it, half).wait_recv()
        return 1.0 / (jnp.sum(rowrecv[it, half], axis=0) + rowbuf[it, half])

    for it in range(ITERS):
        if it > 0:
            for half in (0, 1):
                col_pass(half, row_take(it - 1, half))
        fold(colbuf.at[it])
        col_send(it)
        c16 = TARGET / col_take(it)
        for b in range(LT):
            cb[b * 128 : (b + 1) * 128, :] = spread(c16[b : b + 1, :])
        for half in (0, 1):
            row_send(it, half, row_pass(half))

    last = {}

    def gemm2(groups, parts=4):
        n = ROWS // parts
        total, mass = None, [None] * len(groups)
        for q in range(parts):
            half = q * 2 // parts
            if half not in last:
                last[half] = row_take(ITERS - 1, half)
            first = q * n // 128 - half * HT
            scale = jnp.concatenate([last[half][t : t + 1, :] for t in range(first, first + n // 128)], axis=1)
            plans = []
            for i, (h, step) in enumerate(groups):
                plan = K[pl.ds(group_at(h, step), GROUP), q * n : (q + 1) * n] * scale
                part = [plan[:, t * 128 : (t + 1) * 128] for t in range(n // 128)]
                while len(part) > 1:
                    part = [part[t] + part[t + 1] for t in range(0, len(part), 2)]
                mass[i] = part[0] if mass[i] is None else mass[i] + part[0]
                plans.append(plan.astype(BF16))
            soft = jnp.dot(jnp.concatenate(plans, axis=0), U[q * n : (q + 1) * n, :], preferred_element_type=F32)
            total = soft if total is None else total + soft
        for i, (h, step) in enumerate(groups):
            csum[pl.ds(group_at(h, step), GROUP), :] = mass[i]
        return [total[i * GROUP : (i + 1) * GROUP, :] for i in range(len(groups))]

    HALF = GROUP // 2

    def cols(w):
        return slice(w * WAVE, (w + 1) * WAVE)

    def rs_copy(h, w, way, k):
        lanes = pl.ds(w * WAVE, WAVE)
        if k == 0:
            src, dst = Sb.at[h, 2, pl.ds(way * HALF, HALF), lanes], Rl.at[h, way, :, lanes]
        else:
            half = 1 - way if k == 1 else way
            src, dst = (b.at[h, way, pl.ds(half * HALF, HALF), lanes] for b in (Sb, Sr))
        return remote(
            src, dst, rs_s.at[h, w, way, k], rs_r.at[h, w, way, k], along(h, 1, 1 if way == 0 else 3)
        )

    def rs_add(h, w, way):
        half = pl.ds(way * HALF, HALF)
        rs_copy(h, w, way, 0).wait_recv()
        Sb[h, way, half, cols(w)] = (Acc[h, way, :, cols(w)] + Rl[h, way, :, cols(w)].astype(F32)).astype(BF16)
        rs_copy(h, w, way, 2).start()

    for h, value in enumerate(gemm2([(0, 2), (1, 2)])):
        Sb[h, 2] = value.astype(BF16)
    for w in (0, 1):
        for h in (0, 1):
            for way in (0, 1):
                rs_copy(h, w, way, 0).start()

    for way in (0, 1):
        values = gemm2([(h, 1 if way == 0 else 3) for h in (0, 1)])
        other = 1 - way
        for h in (0, 1):
            Sb[h, way, pl.ds(other * HALF, HALF), :] = values[h][other * HALF : (other + 1) * HALF, :].astype(BF16)
            Acc[h, way] = values[h][way * HALF : (way + 1) * HALF, :]
        for w in (0, 1):
            for h in (0, 1):
                rs_copy(h, w, way, 1).start()
    for h, value in enumerate(gemm2([(0, 0), (1, 0)])):
        Own[h] = value
    for w in (0, 1):
        for way in (0, 1):
            for h in (0, 1):
                rs_add(h, w, way)
    fold(colbuf.at[ITERS])
    col_send(ITERS)

    def r2_copy(h, w, d):
        lanes = pl.ds(w * WAVE, WAVE)
        return remote(
            Tb.at[h, d - 1, :, lanes], Tr.at[h, d - 1, :, lanes],
            r2_s.at[h, w, d - 1], r2_r.at[h, w, d - 1], along(h, 0, d),
        )

    def sub(h, d):
        return pl.ds(pl.multiple_of((place(h, 0)[0] + d) % 4 * SUB, SUB), SUB)

    for w in (0, 1):
        for h in (0, 1):
            for way in (0, 1):
                for k in (1, 2):
                    rs_copy(h, w, way, k).wait_recv()
            Own[h, :, cols(w)] += Sr[h, 0, :, cols(w)].astype(F32) + Sr[h, 1, :, cols(w)].astype(F32)
            for d in (2, 1, 3):
                Tb[h, d - 1, :, cols(w)] = Own[h, sub(h, d), cols(w)].astype(BF16)
                r2_copy(h, w, d).start()

    colbuf[ITERS + 1] = col_take(ITERS)
    held = []
    for h in (0, 1):
        a, b = place(h, 0)
        wt[...] = spread(colbuf[ITERS + 1, pl.ds(h * 4 + b, 1), :])
        wbuf[pl.ds(h * SUB, SUB), :] = wt[pl.ds(pl.multiple_of(a * SUB, SUB), SUB), :]
        scale = cb[pl.ds(pl.multiple_of(h * HALFLISTS + b * GROUP + a * SUB, SUB), SUB), :]
        held.append(wbuf[pl.ds(h * SUB, SUB), :] * scale)
    mass = jnp.concatenate(held + [jnp.zeros((128 - MINE, 128), F32)], axis=0).T[0:8, :]
    mbuf[dp] = mass
    fin_peers = (
        (dev(zh, 1 - zl, x, y, 1 - c), (1 - zl) * 2 + 1 - c),
        (dev(zh, 1 - zl, x, y, c), (1 - zl) * 2 + c),
        (sibling, zl * 2 + 1 - c),
    )

    def mass_copy(k, sent=True):
        slot = mbuf.at[dp if sent else fin_peers[k][1]]
        return remote(slot, slot, m_s.at[k], m_r.at[k], fin_peers[k][0])

    for k in range(3):
        mass_copy(k).start()

    def fin_copy(k, sent=True):
        to = fin_peers[k][1]
        return remote(Fs.at[to if sent else dp], Fr.at[dp if sent else to], fin_s.at[k], fin_r.at[k], fin_peers[k][0])

    for w in (0, 1):
        for h in (0, 1):
            total = Own[h, sub(h, 0), cols(w)]
            for d in (2, 1, 3):
                r2_copy(h, w, d).wait_recv()
                total += Tr[h, d - 1, :, cols(w)].astype(F32)
            weight = 1.0 / wbuf[pl.ds(h * SUB, SUB), :]
            total *= jnp.concatenate([weight] * (WAVE // 128), axis=1)
            for k in (0, 1):
                Fs[2 * w + k, pl.ds(h * SUB, SUB), :] = total[:, k * WIDTH : (k + 1) * WIDTH].astype(Fs.dtype)
    for k in range(3):
        fin_copy(k).start()

    for k in range(3):
        mass_copy(k, False).wait_recv()
    for k in (0, 1):
        mass_ref[k : k + 1, :] = jnp.concatenate([mbuf[2 * k, 0:1, 0:MINE], mbuf[2 * k + 1, 0:1, 0:MINE]], axis=1)

    mass_out = pltpu.make_async_copy(mass_ref, mass_hbm, out_s.at[1])
    mass_out.start()
    Fr[dp] = Fs[dp]
    for k in (2, 1, 0):
        fin_copy(k, False).wait_recv()
    for k in (0, 1):
        value = jnp.concatenate([Fr[2 * k], Fr[2 * k + 1]], axis=0).astype(F32)
        out_ref[0:128, k * 128 : (k + 1) * 128] = value[:, 0:128].T
        side = jnp.concatenate([value[:, 128:192], jnp.zeros((128, 64), F32)], axis=1)
        out_ref[128:192, k * 128 : (k + 1) * 128] = side.T[0:64, :]

    new_out = pltpu.make_async_copy(out_ref, out_hbm, out_s.at[0])
    new_out.start()

    for h in (0, 1):
        for d in (1, 2, 3):
            a0_copy(h, d).wait_send()
            for w in (0, 1):
                r2_copy(h, w, d).wait_send()
        for way in (0, 1):
            for k in (0, 1, 2):
                for j in range(4):
                    a1_copy(h, j, way, k).wait_send()
                for w in (0, 1):
                    rs_copy(h, w, way, k).wait_send()
    for k in range(chunks):
        for way in (0, 1):
            p_z(k, way).wait_send()
        p_sib(k).wait_send()
        p_relay(k).wait_send()
        for d in (1, 2, 3):
            p_fwd(d, k).wait_send()
    for it in range(ITERS + 1):
        col_all(it).wait_send()
    for it in range(ITERS):
        for half in (0, 1):
            row_all(it, half).wait_send()
    for k in range(3):
        mass_copy(k).wait_send()
        fin_copy(k).wait_send()
    mass_out.wait()
    new_out.wait()


def on_device(passages, centroids):
    lists = centroids.shape[0]
    chunks = OWN // CHUNK
    dma = pltpu.SemaphoreType.DMA
    vm = pltpu.VMEM
    new, mass = pl.pallas_call(
        body,
        out_shape=(
            jax.ShapeDtypeStruct((WIDTH, lists), F32),
            jax.ShapeDtypeStruct((2, 128), F32),
        ),
        in_specs=[pl.BlockSpec(memory_space=pl.ANY)] * 2,
        out_specs=(pl.BlockSpec(memory_space=pl.ANY),) * 2,
        scratch_shapes=[
            vm((WIDTH, lists), F32),
            vm((2, 128), F32),
            vm((OWN, D), BF16),
            vm((MINE, D), BF16),
            vm((ROWS, D), BF16),
            vm((LISTS, D), BF16),
            vm((LISTS, ROWS), F32),
            vm((LISTS, 128), F32),
            vm((LISTS, 128), F32),
            vm((ITERS + 2, LT, 128), F32),
            vm((ITERS + 1, len(PEERS), LT, 128), F32),
            vm((ITERS, 2, HT, 128), F32),
            vm((ITERS, 2, 7, HT, 128), F32),
            vm((2, 3, GROUP, D), BF16),
            vm((2, 2, GROUP, D), BF16),
            vm((2, 2, GROUP // 2, D), BF16),
            vm((2, 2, GROUP // 2, D), F32),
            vm((2, GROUP, D), F32),
            vm((2, 3, SUB, D), BF16),
            vm((2, 3, SUB, D), BF16),
            vm((4, MINE, WIDTH), BF16),
            vm((4, MINE, WIDTH), BF16),
            vm((128, 128), F32),
            vm((MINE, 128), F32),
            vm((4, 8, 128), F32),
            dma((2,)),
            dma((2,)),
            dma((2, 3)), dma((2, 3)),
            dma((2, 4, 2, 3)), dma((2, 4, 2, 3)),
            dma((chunks,)), dma((chunks,)),
            dma((2, chunks)), dma((2, chunks)),
            dma((chunks,)), dma((chunks,)),
            dma((3, chunks)), dma((3, chunks)),
            dma((ITERS + 1,)), dma((ITERS + 1,)),
            dma((ITERS, 2)), dma((ITERS, 2)),
            dma((2, 2, 2, 3)), dma((2, 2, 2, 3)),
            dma((2, 2, 3)), dma((2, 2, 3)),
            dma((3,)), dma((3,)),
            dma((3,)), dma((3,)),
        ],
        compiler_params=pltpu.CompilerParams(
            collective_id=0, has_side_effects=True, vmem_limit_bytes=60 * 1024 * 1024
        ),
        cost_estimate=pl.CostEstimate(
            flops=4 * LISTS * ROWS * D, bytes_accessed=2 * 1024 * 1024, transcendentals=LISTS * ROWS
        ),
        name="sinkhorn",
    )(passages, centroids)
    return new.T, mass.reshape(lists)


def solution(mesh):
    return jax.shard_map(
        on_device,
        mesh=mesh,
        in_specs=(P(("dp", "list"), None), P("list", None)),
        out_specs=(P("list", "dp"), P("list")),
        check_vma=False,
    )
```

```python
import jax
import jax.numpy as jnp
from jax import lax
from jax.experimental import pallas as pl
from jax.experimental.pallas import tpu as pltpu
from jax.sharding import PartitionSpec as P

MESH = pl.DeviceIdType.MESH
F32 = jnp.float32
BF16 = jnp.bfloat16

ITERS = 3
D = 768
LISTS = 1024
ROWS = 4096
OWN = 512
CHUNK = 128
GROUP = 128
SUB = 32
HALFLISTS = LISTS // 2
MINE = 2 * SUB
LT = LISTS // 128
RT = ROWS // 128
HT = RT // 2
TARGET = 8.0
LOG2E20 = 20.0 * 1.4426950408889634

WIDTH = D // 4
WAVE = D // 2


def far_first():
    deltas = [(a, b) for a in range(4) for b in range(4) if (a, b) != (0, 0)]
    return tuple(sorted(deltas, key=lambda d: -(min(d[0], 4 - d[0]) + min(d[1], 4 - d[1]))))


PEERS = far_first()


def unit(values):
    wide = values.astype(F32)
    return (wide * lax.rsqrt(jnp.sum(wide * wide, axis=-1, keepdims=True) + 1e-06)).astype(BF16)


def spread(row):
    return jnp.broadcast_to(row, (128, 128)).T


def body(
    p_hbm, cent_hbm, out_hbm, mass_hbm,
    out_ref, mass_ref,
    P_in, C_in, U, C, K, csum, cb, colbuf, colrecv, rowbuf, rowrecv,
    Sb, Sr, Rl, Acc, Own, Tb, Tr, Fs, Fr, wt, wbuf, mbuf,
    in_s, out_s, a0_s, a0_r, a1_s, a1_r, ps_s, ps_r, pz_s, pz_r, pr_s, pr_r, pf_s, pf_r, col_s, col_r, row_s, row_r,
    rs_s, rs_r, r2_s, r2_r, fin_s, fin_r, m_s, m_r,
):
    dp = lax.axis_index("dp")
    li = lax.axis_index("list")
    zl, c = dp // 2, dp % 2
    zh, x, y = li // 16, (li // 4) % 4, li % 4

    def dev(zh_, zl_, x_, y_, c_):
        return (zl_ * 2 + c_, zh_ * 16 + x_ * 4 + y_)

    z = zh * 2 + zl
    sibling = dev(zh, zl, x, y, 1 - c)

    def up(d, core):
        to = (z + d) % 4
        return dev(to // 2, to % 2, x, y, core)

    def near(dx, dy):
        return dev(zh, zl, (x + dx) % 4, (y + dy) % 4, c)

    peers = [near(d, 0) for d in (1, 2, 3)] + [near(0, d) for d in (1, 2, 3)]
    peers += [up(1, c), up(3, c), sibling]
    barrier = pltpu.get_barrier_semaphore()
    for peer in peers:
        pl.semaphore_signal(barrier, inc=1, device_id=peer, device_id_type=MESH)

    def remote(src, dst, send, recv, device):
        return pltpu.make_async_remote_copy(
            src_ref=src, dst_ref=dst, send_sem=send, recv_sem=recv,
            device_id=device, device_id_type=MESH,
        )

    p_in = pltpu.make_async_copy(p_hbm, P_in, in_s.at[0])
    c_in = pltpu.make_async_copy(cent_hbm.at[pl.ds(pl.multiple_of(dp * MINE, MINE), MINE), :], C_in, in_s.at[1])
    p_in.start()
    c_in.start()

    def along(h, phase, step):
        if (h + phase) % 2 == 0:
            return near(step, 0)
        return near(0, step)

    def place(h, phase):
        return (x, y) if (h + phase) % 2 == 0 else (y, x)

    def block(h, a, b, part, parts):
        n = SUB // parts
        at = h * HALFLISTS + b * GROUP + a * SUB + part * n
        return C.at[pl.ds(pl.multiple_of(at, n), n), :]

    def a0_copy(h, d, sent=True):
        a, b = place(h, 0)
        ref = block(h, a if sent else (a + 4 - d) % 4, b, 0, 1)
        return remote(ref, ref, a0_s.at[h, d - 1], a0_r.at[h, d - 1], along(h, 0, d))

    def a1_copy(h, j, way, k, sent=True):
        a, b = place(h, 0)
        back = (3 if way == 0 else 1)
        src = b if sent else (b + back) % 4
        if k == 2:
            src = (b + (back if sent else 2)) % 4
        half = way if k != 1 else 1 - way
        ref = block(h, (a + 4 - j) % 4, src, half, 2)
        return remote(
            ref, ref, a1_s.at[h, j, way, k], a1_r.at[h, j, way, k], along(h, 1, 1 if way == 0 else 3)
        )

    def a1_start(j, k):
        for h in (0, 1):
            for way in (0, 1):
                a1_copy(h, j, way, k).start()

    def a1_relay(j):
        for h in (0, 1):
            for way in (0, 1):
                a1_copy(h, j, way, 0, False).wait_recv()
                a1_copy(h, j, way, 2).start()

    def a1_wait(j, k):
        for h in (0, 1):
            for way in (0, 1):
                a1_copy(h, j, way, k, False).wait_recv()

    def rows(at, k, core):
        return pl.ds(pl.multiple_of(at * 1024 + k * 256 + core * CHUNK, CHUNK), CHUNK)

    chunks = OWN // CHUNK

    def p_copy(d, core, k, send, recv, device):
        ref = U.at[rows((z + d) % 4, k, core), :]
        return remote(ref, ref, send, recv, device)

    def p_sib(k, sent=True):
        return p_copy(0, c if sent else 1 - c, k, ps_s.at[k], ps_r.at[k], sibling)

    def p_z(k, way, sent=True):
        step = 1 if way == 0 else 3
        return p_copy(0 if sent else 4 - step, c, k, pz_s.at[way, k], pz_r.at[way, k], up(step, c))

    def p_relay(k, sent=True):
        step = 1 if k < 2 else 3
        return p_copy(4 - step if sent else 2, c, k, pr_s.at[k], pr_r.at[k], up(step, c))

    def p_fwd(d, k, sent=True):
        return p_copy(d, c if sent else 1 - c, k, pf_s.at[d - 1, k], pf_r.at[d - 1, k], sibling)

    def p_near(way, k):
        p_z(k, way, False).wait_recv()
        if (k < 2) == (way == 0):
            p_relay(k).start()
        p_fwd(3 if way == 0 else 1, k).start()

    def p_far(k):
        p_relay(k, False).wait_recv()
        p_fwd(2, k).start()

    p_in.wait()
    for k in range(chunks):
        U[rows(z, k, c), :] = unit(P_in[pl.ds(k * CHUNK, CHUNK), :])
    c_in.wait()
    for h in (0, 1):
        a, b = place(h, 0)
        at = pl.multiple_of(h * HALFLISTS + b * GROUP + a * SUB, SUB)
        C[pl.ds(at, SUB), :] = unit(C_in[pl.ds(h * SUB, SUB), :])

    pl.semaphore_wait(barrier, len(peers))
    for way in (0, 1):
        p_z(2 * way, way).start()
    for h in (0, 1):
        for d in (1, 3):
            a0_copy(h, d).start()
    for h in (0, 1):
        a0_copy(h, 2).start()
    a1_start(0, 0)
    for k in range(chunks):
        p_sib(k).start()
    for k in (1, 2, 3):
        for way in (0, 1):
            p_z((k + 2 * way) % 4, way).start()

    def gemm1(at, m, qt, n, first):
        s = lax.dot_general(
            C[pl.ds(at, m), :], U[pl.ds(qt, n), :],
            (((1,), (1,)), ((), ())), preferred_element_type=F32,
        )
        e = jnp.exp2(s * LOG2E20)
        K[pl.ds(at, m), pl.ds(qt, n)] = e
        part = [e[:, t * 128 : (t + 1) * 128] for t in range(n // 128)]
        while len(part) > 1:
            part = [part[t] + part[t + 1] for t in range(0, len(part), 2)]
        csum[pl.ds(at, m), :] = part[0] if first else csum[pl.ds(at, m), :] + part[0]

    def group_at(h, step):
        return pl.multiple_of(h * HALFLISTS + (place(h, 1)[0] + step) % 4 * GROUP, GROUP)

    def own_gemm():
        for g in range(0, LISTS, 256):
            gemm1(g, 256, pl.multiple_of(z * 1024, 1024), 1024, True)

    def far_gemm(d, k):
        at = pl.multiple_of((z + d) % 4 * 1024 + k * 256, 256)
        for g in range(0, LISTS, 256):
            gemm1(g, 256, at, 256, False)

    def a0_wait(d):
        for h in (0, 1):
            a0_copy(h, d, False).wait_recv()

    a0_wait(1)
    a1_start(1, 0)
    a0_wait(3)
    a1_start(3, 0)
    a1_start(0, 1)
    a0_wait(2)
    a1_start(2, 0)
    for j in (1, 3, 2):
        a1_start(j, 1)
    a1_relay(0)
    for k in range(chunks):
        p_sib(k, False).wait_recv()
    p_near(0, 0)
    p_near(1, 2)
    a1_relay(1)
    a1_relay(3)
    a1_relay(2)
    p_near(0, 1)
    p_near(1, 3)
    for k in (1, 2):
        for j in (0, 1, 3, 2):
            a1_wait(j, k)
    own_gemm()

    def far(d, k):
        p_fwd(d, k, False).wait_recv()
        far_gemm(d, k)

    p_near(0, 2)
    p_near(1, 0)
    far(3, 0)
    far(1, 2)
    far(3, 1)
    far(1, 3)
    p_near(0, 3)
    p_near(1, 1)
    far(3, 2)
    far(1, 0)
    p_far(0)
    p_far(2)
    far(3, 3)
    far(1, 1)
    far(2, 0)
    far(2, 2)
    p_far(1)
    p_far(3)
    far(2, 1)
    far(2, 3)

    def col_pass(half, r16):
        strips = 32

        @pl.loop(0, LISTS // (8 * strips))
        def _(i):
            acc = [None] * strips
            for t in range(HT):
                r = jnp.broadcast_to(r16[t : t + 1, :], (8, 128))
                lanes = slice((half * HT + t) * 128, (half * HT + t + 1) * 128)
                for s in range(strips):
                    at = pl.multiple_of(i * (8 * strips) + s * 8, 8)
                    term = K[pl.ds(at, 8), lanes] * r
                    if t == 0 and half == 1:
                        term += csum[pl.ds(at, 8), :]
                    acc[s] = term if acc[s] is None else acc[s] + term
            for s in range(strips):
                csum[pl.ds(pl.multiple_of(i * (8 * strips) + s * 8, 8), 8), :] = acc[s]

    def fold(out):
        parts = []
        for b in range(LT):
            square = csum[b * 128 : (b + 1) * 128, :]
            parts.append(jnp.sum(square.T, axis=0, keepdims=True))
        out[...] = jnp.concatenate(parts, axis=0)

    def col_send(it):
        for k, delta in enumerate(PEERS):
            remote(colbuf.at[it], colrecv.at[it, k], col_s.at[it], col_r.at[it], near(*delta)).start()

    def col_all(it):
        return remote(colrecv.at[it], colrecv.at[it], col_s.at[it], col_r.at[it], near(*PEERS[0]))

    def col_take(it):
        col_all(it).wait_recv()
        return jnp.sum(colrecv[it], axis=0) + colbuf[it]

    def row_pass(half):
        def step(i, acc):
            acc = list(acc)
            for s in range(8):
                at = pl.multiple_of(i * 64 + s * 8, 8)
                scale = cb[pl.ds(at, 8), :]
                for t in range(HT):
                    acc[t] += K[pl.ds(at, 8), (half * HT + t) * 128 : (half * HT + t + 1) * 128] * scale
            return tuple(acc)

        zero = tuple(jnp.zeros((8, 128), F32) for _ in range(HT))
        acc = lax.fori_loop(0, LISTS // 64, step, zero)
        return jnp.concatenate([jnp.sum(a, axis=0, keepdims=True) for a in acc], axis=0)

    row_peers = [up(2, 1 - c), up(2, c)] + [up(d, 1 - c) for d in (1, 3)] + [up(d, c) for d in (1, 3)] + [sibling]

    def row_send(it, half, value):
        rowbuf[it, half] = value
        for k, peer in enumerate(row_peers):
            remote(
                rowbuf.at[it, half], rowrecv.at[it, half, k], row_s.at[it, half], row_r.at[it, half], peer
            ).start()

    def row_all(it, half):
        got = rowrecv.at[it, half]
        return remote(got, got, row_s.at[it, half], row_r.at[it, half], sibling)

    def row_take(it, half):
        row_all(it, half).wait_recv()
        return 1.0 / (jnp.sum(rowrecv[it, half], axis=0) + rowbuf[it, half])

    for it in range(ITERS):
        if it > 0:
            for half in (0, 1):
                col_pass(half, row_take(it - 1, half))
        fold(colbuf.at[it])
        col_send(it)
        c16 = TARGET / col_take(it)
        for b in range(LT):
            cb[b * 128 : (b + 1) * 128, :] = spread(c16[b : b + 1, :])
        for half in (0, 1):
            row_send(it, half, row_pass(half))

    last = {}

    def gemm2(groups, parts=4):
        n = ROWS // parts
        total, mass = None, [None] * len(groups)
        for q in range(parts):
            half = q * 2 // parts
            if half not in last:
                last[half] = row_take(ITERS - 1, half)
            first = q * n // 128 - half * HT
            scale = jnp.concatenate([last[half][t : t + 1, :] for t in range(first, first + n // 128)], axis=1)
            plans = []
            for i, (h, step) in enumerate(groups):
                plan = K[pl.ds(group_at(h, step), GROUP), q * n : (q + 1) * n] * scale
                part = [plan[:, t * 128 : (t + 1) * 128] for t in range(n // 128)]
                while len(part) > 1:
                    part = [part[t] + part[t + 1] for t in range(0, len(part), 2)]
                mass[i] = part[0] if mass[i] is None else mass[i] + part[0]
                plans.append(plan.astype(BF16))
            soft = jnp.dot(jnp.concatenate(plans, axis=0), U[q * n : (q + 1) * n, :], preferred_element_type=F32)
            total = soft if total is None else total + soft
        for i, (h, step) in enumerate(groups):
            csum[pl.ds(group_at(h, step), GROUP), :] = mass[i]
        return [total[i * GROUP : (i + 1) * GROUP, :] for i in range(len(groups))]

    HALF = GROUP // 2

    def cols(w):
        return slice(w * WAVE, (w + 1) * WAVE)

    def rs_copy(h, w, way, k):
        lanes = pl.ds(w * WAVE, WAVE)
        if k == 0:
            src, dst = Sb.at[h, 2, pl.ds(way * HALF, HALF), lanes], Rl.at[h, way, :, lanes]
        else:
            half = 1 - way if k == 1 else way
            src, dst = (b.at[h, way, pl.ds(half * HALF, HALF), lanes] for b in (Sb, Sr))
        return remote(
            src, dst, rs_s.at[h, w, way, k], rs_r.at[h, w, way, k], along(h, 1, 1 if way == 0 else 3)
        )

    def rs_add(h, w, way):
        half = pl.ds(way * HALF, HALF)
        rs_copy(h, w, way, 0).wait_recv()
        Sb[h, way, half, cols(w)] = (Acc[h, way, :, cols(w)] + Rl[h, way, :, cols(w)].astype(F32)).astype(BF16)
        rs_copy(h, w, way, 2).start()

    for h, value in enumerate(gemm2([(0, 2), (1, 2)])):
        Sb[h, 2] = value.astype(BF16)
    for w in (0, 1):
        for h in (0, 1):
            for way in (0, 1):
                rs_copy(h, w, way, 0).start()

    for way in (0, 1):
        values = gemm2([(h, 1 if way == 0 else 3) for h in (0, 1)])
        other = 1 - way
        for h in (0, 1):
            Sb[h, way, pl.ds(other * HALF, HALF), :] = values[h][other * HALF : (other + 1) * HALF, :].astype(BF16)
            Acc[h, way] = values[h][way * HALF : (way + 1) * HALF, :]
        for w in (0, 1):
            for h in (0, 1):
                rs_copy(h, w, way, 1).start()
    for h, value in enumerate(gemm2([(0, 0), (1, 0)])):
        Own[h] = value
    for w in (0, 1):
        for way in (0, 1):
            for h in (0, 1):
                rs_add(h, w, way)
    fold(colbuf.at[ITERS])
    col_send(ITERS)

    def r2_copy(h, w, d):
        lanes = pl.ds(w * WAVE, WAVE)
        return remote(
            Tb.at[h, d - 1, :, lanes], Tr.at[h, d - 1, :, lanes],
            r2_s.at[h, w, d - 1], r2_r.at[h, w, d - 1], along(h, 0, d),
        )

    def sub(h, d):
        return pl.ds(pl.multiple_of((place(h, 0)[0] + d) % 4 * SUB, SUB), SUB)

    for w in (0, 1):
        for h in (0, 1):
            for way in (0, 1):
                for k in (1, 2):
                    rs_copy(h, w, way, k).wait_recv()
            Own[h, :, cols(w)] += Sr[h, 0, :, cols(w)].astype(F32) + Sr[h, 1, :, cols(w)].astype(F32)
            for d in (2, 1, 3):
                Tb[h, d - 1, :, cols(w)] = Own[h, sub(h, d), cols(w)].astype(BF16)
                r2_copy(h, w, d).start()

    colbuf[ITERS + 1] = col_take(ITERS)
    held = []
    for h in (0, 1):
        a, b = place(h, 0)
        wt[...] = spread(colbuf[ITERS + 1, pl.ds(h * 4 + b, 1), :])
        wbuf[pl.ds(h * SUB, SUB), :] = wt[pl.ds(pl.multiple_of(a * SUB, SUB), SUB), :]
        scale = cb[pl.ds(pl.multiple_of(h * HALFLISTS + b * GROUP + a * SUB, SUB), SUB), :]
        held.append(wbuf[pl.ds(h * SUB, SUB), :] * scale)
    mass = jnp.concatenate(held + [jnp.zeros((128 - MINE, 128), F32)], axis=0).T[0:8, :]
    mbuf[dp] = mass
    fin_peers = (
        (dev(zh, 1 - zl, x, y, 1 - c), (1 - zl) * 2 + 1 - c),
        (dev(zh, 1 - zl, x, y, c), (1 - zl) * 2 + c),
        (sibling, zl * 2 + 1 - c),
    )

    def mass_copy(k, sent=True):
        slot = mbuf.at[dp if sent else fin_peers[k][1]]
        return remote(slot, slot, m_s.at[k], m_r.at[k], fin_peers[k][0])

    for k in range(3):
        mass_copy(k).start()

    def fin_copy(k, sent=True):
        to = fin_peers[k][1]
        return remote(Fs.at[to if sent else dp], Fr.at[dp if sent else to], fin_s.at[k], fin_r.at[k], fin_peers[k][0])

    for w in (0, 1):
        for h in (0, 1):
            total = Own[h, sub(h, 0), cols(w)]
            for d in (2, 1, 3):
                r2_copy(h, w, d).wait_recv()
                total += Tr[h, d - 1, :, cols(w)].astype(F32)
            weight = 1.0 / wbuf[pl.ds(h * SUB, SUB), :]
            total *= jnp.concatenate([weight] * (WAVE // 128), axis=1)
            for k in (0, 1):
                Fs[2 * w + k, pl.ds(h * SUB, SUB), :] = total[:, k * WIDTH : (k + 1) * WIDTH].astype(Fs.dtype)
    for k in range(3):
        fin_copy(k).start()

    for k in range(3):
        mass_copy(k, False).wait_recv()
    for k in (0, 1):
        mass_ref[k : k + 1, :] = jnp.concatenate([mbuf[2 * k, 0:1, 0:MINE], mbuf[2 * k + 1, 0:1, 0:MINE]], axis=1)

    mass_out = pltpu.make_async_copy(mass_ref, mass_hbm, out_s.at[1])
    mass_out.start()
    Fr[dp] = Fs[dp]
    for k in (2, 1, 0):
        fin_copy(k, False).wait_recv()
    for k in (0, 1):
        value = jnp.concatenate([Fr[2 * k], Fr[2 * k + 1]], axis=0).astype(F32)
        out_ref[0:128, k * 128 : (k + 1) * 128] = value[:, 0:128].T
        side = jnp.concatenate([value[:, 128:192], jnp.zeros((128, 64), F32)], axis=1)
        out_ref[128:192, k * 128 : (k + 1) * 128] = side.T[0:64, :]

    new_out = pltpu.make_async_copy(out_ref, out_hbm, out_s.at[0])
    new_out.start()

    for h in (0, 1):
        for d in (1, 2, 3):
            a0_copy(h, d).wait_send()
            for w in (0, 1):
                r2_copy(h, w, d).wait_send()
        for way in (0, 1):
            for k in (0, 1, 2):
                for j in range(4):
                    a1_copy(h, j, way, k).wait_send()
                for w in (0, 1):
                    rs_copy(h, w, way, k).wait_send()
    for k in range(chunks):
        for way in (0, 1):
            p_z(k, way).wait_send()
        p_sib(k).wait_send()
        p_relay(k).wait_send()
        for d in (1, 2, 3):
            p_fwd(d, k).wait_send()
    for it in range(ITERS + 1):
        col_all(it).wait_send()
    for it in range(ITERS):
        for half in (0, 1):
            row_all(it, half).wait_send()
    for k in range(3):
        mass_copy(k).wait_send()
        fin_copy(k).wait_send()
    mass_out.wait()
    new_out.wait()


def on_device(passages, centroids):
    lists = centroids.shape[0]
    chunks = OWN // CHUNK
    dma = pltpu.SemaphoreType.DMA
    vm = pltpu.VMEM
    new, mass = pl.pallas_call(
        body,
        out_shape=(
            jax.ShapeDtypeStruct((WIDTH, lists), F32),
            jax.ShapeDtypeStruct((2, 128), F32),
        ),
        in_specs=[pl.BlockSpec(memory_space=pltpu.HBM)] * 2,
        out_specs=(pl.BlockSpec(memory_space=pl.ANY),) * 2,
        scratch_shapes=[
            vm((WIDTH, lists), F32),
            vm((2, 128), F32),
            vm((OWN, D), BF16),
            vm((MINE, D), BF16),
            vm((ROWS, D), BF16),
            vm((LISTS, D), BF16),
            vm((LISTS, ROWS), F32),
            vm((LISTS, 128), F32),
            vm((LISTS, 128), F32),
            vm((ITERS + 2, LT, 128), F32),
            vm((ITERS + 1, len(PEERS), LT, 128), F32),
            vm((ITERS, 2, HT, 128), F32),
            vm((ITERS, 2, 7, HT, 128), F32),
            vm((2, 3, GROUP, D), BF16),
            vm((2, 2, GROUP, D), BF16),
            vm((2, 2, GROUP // 2, D), BF16),
            vm((2, 2, GROUP // 2, D), F32),
            vm((2, GROUP, D), F32),
            vm((2, 3, SUB, D), BF16),
            vm((2, 3, SUB, D), BF16),
            vm((4, MINE, WIDTH), BF16),
            vm((4, MINE, WIDTH), BF16),
            vm((128, 128), F32),
            vm((MINE, 128), F32),
            vm((4, 8, 128), F32),
            dma((2,)),
            dma((2,)),
            dma((2, 3)), dma((2, 3)),
            dma((2, 4, 2, 3)), dma((2, 4, 2, 3)),
            dma((chunks,)), dma((chunks,)),
            dma((2, chunks)), dma((2, chunks)),
            dma((chunks,)), dma((chunks,)),
            dma((3, chunks)), dma((3, chunks)),
            dma((ITERS + 1,)), dma((ITERS + 1,)),
            dma((ITERS, 2)), dma((ITERS, 2)),
            dma((2, 2, 2, 3)), dma((2, 2, 2, 3)),
            dma((2, 2, 3)), dma((2, 2, 3)),
            dma((3,)), dma((3,)),
            dma((3,)), dma((3,)),
        ],
        compiler_params=pltpu.CompilerParams(
            collective_id=0, has_side_effects=True, vmem_limit_bytes=48 * 1024 * 1024
        ),
        cost_estimate=pl.CostEstimate(
            flops=4 * LISTS * ROWS * D, bytes_accessed=2 * 1024 * 1024, transcendentals=LISTS * ROWS
        ),
        name="sinkhorn",
    )(passages, centroids)
    return new.T, mass.reshape(lists)


def solution(mesh):
    return jax.shard_map(
        on_device,
        mesh=mesh,
        in_specs=(P(("dp", "list"), None), P("list", None)),
        out_specs=(P("list", "dp"), P("list")),
        check_vma=False,
    )
```

```python
import jax
import jax.numpy as jnp
from jax import lax
from jax.experimental import pallas as pl
from jax.experimental.pallas import tpu as pltpu
from jax.sharding import PartitionSpec as P

MESH = pl.DeviceIdType.MESH
F32 = jnp.float32
BF16 = jnp.bfloat16

ITERS = 3
D = 768
LISTS = 1024
ROWS = 4096
OWN = 512
CHUNK = 128
GROUP = 128
SUB = 32
HALFLISTS = LISTS // 2
MINE = 2 * SUB
LT = LISTS // 128
RT = ROWS // 128
HT = RT // 2
TARGET = 8.0
LOG2E20 = 20.0 * 1.4426950408889634

WIDTH = D // 4
WAVE = D // 2


def far_first():
    deltas = [(a, b) for a in range(4) for b in range(4) if (a, b) != (0, 0)]
    return tuple(sorted(deltas, key=lambda d: -(min(d[0], 4 - d[0]) + min(d[1], 4 - d[1]))))


PEERS = far_first()


def unit(values):
    wide = values.astype(F32)
    return (wide * lax.rsqrt(jnp.sum(wide * wide, axis=-1, keepdims=True) + 1e-06)).astype(BF16)


def spread(row):
    return jnp.broadcast_to(row, (128, 128)).T


def body(
    p_hbm, cent_hbm, out_hbm, mass_hbm,
    out_ref, mass_ref,
    P_in, C_in, U, C, K, csum, cb, colbuf, colrecv, rowbuf, rowrecv,
    Sb, Sr, Rl, Acc, Own, Tb, Tr, Fs, Fr, wt, wbuf, mbuf,
    in_s, out_s, a0_s, a0_r, a1_s, a1_r, ps_s, ps_r, pz_s, pz_r, pr_s, pr_r, pf_s, pf_r, col_s, col_r, row_s, row_r,
    rs_s, rs_r, r2_s, r2_r, fin_s, fin_r, m_s, m_r,
):
    dp = lax.axis_index("dp")
    li = lax.axis_index("list")
    zl, c = dp // 2, dp % 2
    zh, x, y = li // 16, (li // 4) % 4, li % 4

    def dev(zh_, zl_, x_, y_, c_):
        return (zl_ * 2 + c_, zh_ * 16 + x_ * 4 + y_)

    z = zh * 2 + zl
    sibling = dev(zh, zl, x, y, 1 - c)

    def up(d, core):
        to = (z + d) % 4
        return dev(to // 2, to % 2, x, y, core)

    def near(dx, dy):
        return dev(zh, zl, (x + dx) % 4, (y + dy) % 4, c)

    peers = [near(d, 0) for d in (1, 2, 3)] + [near(0, d) for d in (1, 2, 3)]
    peers += [up(1, c), up(3, c), sibling]
    barrier = pltpu.get_barrier_semaphore()
    for peer in peers:
        pl.semaphore_signal(barrier, inc=1, device_id=peer, device_id_type=MESH)

    def remote(src, dst, send, recv, device):
        return pltpu.make_async_remote_copy(
            src_ref=src, dst_ref=dst, send_sem=send, recv_sem=recv,
            device_id=device, device_id_type=MESH,
        )

    p_in = pltpu.make_async_copy(p_hbm, P_in, in_s.at[0])
    c_in = pltpu.make_async_copy(cent_hbm.at[pl.ds(pl.multiple_of(dp * MINE, MINE), MINE), :], C_in, in_s.at[1])
    p_in.start()
    c_in.start()

    def along(h, phase, step):
        if (h + phase) % 2 == 0:
            return near(step, 0)
        return near(0, step)

    def place(h, phase):
        return (x, y) if (h + phase) % 2 == 0 else (y, x)

    def block(h, a, b, part, parts):
        n = SUB // parts
        at = h * HALFLISTS + b * GROUP + a * SUB + part * n
        return C.at[pl.ds(pl.multiple_of(at, n), n), :]

    def a0_copy(h, d, sent=True):
        a, b = place(h, 0)
        ref = block(h, a if sent else (a + 4 - d) % 4, b, 0, 1)
        return remote(ref, ref, a0_s.at[h, d - 1], a0_r.at[h, d - 1], along(h, 0, d))

    def a1_copy(h, j, way, k, sent=True):
        a, b = place(h, 0)
        back = (3 if way == 0 else 1)
        src = b if sent else (b + back) % 4
        if k == 2:
            src = (b + (back if sent else 2)) % 4
        half = way if k != 1 else 1 - way
        ref = block(h, (a + 4 - j) % 4, src, half, 2)
        return remote(
            ref, ref, a1_s.at[h, j, way, k], a1_r.at[h, j, way, k], along(h, 1, 1 if way == 0 else 3)
        )

    def a1_start(j, k):
        for h in (0, 1):
            for way in (0, 1):
                a1_copy(h, j, way, k).start()

    def a1_relay(j):
        for h in (0, 1):
            for way in (0, 1):
                a1_copy(h, j, way, 0, False).wait_recv()
                a1_copy(h, j, way, 2).start()

    def a1_wait(j, k):
        for h in (0, 1):
            for way in (0, 1):
                a1_copy(h, j, way, k, False).wait_recv()

    def rows(at, k, core):
        return pl.ds(pl.multiple_of(at * 1024 + k * 256 + core * CHUNK, CHUNK), CHUNK)

    chunks = OWN // CHUNK

    def p_copy(d, core, k, send, recv, device):
        ref = U.at[rows((z + d) % 4, k, core), :]
        return remote(ref, ref, send, recv, device)

    def p_sib(k, sent=True):
        return p_copy(0, c if sent else 1 - c, k, ps_s.at[k], ps_r.at[k], sibling)

    def p_z(k, way, sent=True):
        step = 1 if way == 0 else 3
        return p_copy(0 if sent else 4 - step, c, k, pz_s.at[way, k], pz_r.at[way, k], up(step, c))

    def p_relay(k, sent=True):
        step = 1 if k < 2 else 3
        return p_copy(4 - step if sent else 2, c, k, pr_s.at[k], pr_r.at[k], up(step, c))

    def p_fwd(d, k, sent=True):
        return p_copy(d, c if sent else 1 - c, k, pf_s.at[d - 1, k], pf_r.at[d - 1, k], sibling)

    def p_near(way, k):
        p_z(k, way, False).wait_recv()
        if (k < 2) == (way == 0):
            p_relay(k).start()
        p_fwd(3 if way == 0 else 1, k).start()

    def p_far(k):
        p_relay(k, False).wait_recv()
        p_fwd(2, k).start()

    p_in.wait()
    for k in range(chunks):
        U[rows(z, k, c), :] = unit(P_in[pl.ds(k * CHUNK, CHUNK), :])
    c_in.wait()
    for h in (0, 1):
        a, b = place(h, 0)
        at = pl.multiple_of(h * HALFLISTS + b * GROUP + a * SUB, SUB)
        C[pl.ds(at, SUB), :] = unit(C_in[pl.ds(h * SUB, SUB), :])

    pl.semaphore_wait(barrier, len(peers))
    for way in (0, 1):
        p_z(2 * way, way).start()
    for h in (0, 1):
        for d in (1, 3):
            a0_copy(h, d).start()
    for h in (0, 1):
        a0_copy(h, 2).start()
    a1_start(0, 0)
    for k in range(chunks):
        p_sib(k).start()
    for k in (1, 2, 3):
        for way in (0, 1):
            p_z((k + 2 * way) % 4, way).start()

    def gemm1(at, m, qt, n, first):
        s = lax.dot_general(
            C[pl.ds(at, m), :], U[pl.ds(qt, n), :],
            (((1,), (1,)), ((), ())), preferred_element_type=F32,
        )
        e = jnp.exp2(s * LOG2E20)
        K[pl.ds(at, m), pl.ds(qt, n)] = e
        part = [e[:, t * 128 : (t + 1) * 128] for t in range(n // 128)]
        while len(part) > 1:
            part = [part[t] + part[t + 1] for t in range(0, len(part), 2)]
        csum[pl.ds(at, m), :] = part[0] if first else csum[pl.ds(at, m), :] + part[0]

    def group_at(h, step):
        return pl.multiple_of(h * HALFLISTS + (place(h, 1)[0] + step) % 4 * GROUP, GROUP)

    def own_gemm():
        for g in range(0, LISTS, 256):
            gemm1(g, 256, pl.multiple_of(z * 1024, 1024), 1024, True)

    def far_gemm(d, k):
        at = pl.multiple_of((z + d) % 4 * 1024 + k * 256, 256)
        for g in range(0, LISTS, 256):
            gemm1(g, 256, at, 256, False)

    def a0_wait(d):
        for h in (0, 1):
            a0_copy(h, d, False).wait_recv()

    a0_wait(1)
    a1_start(1, 0)
    a0_wait(3)
    a1_start(3, 0)
    a1_start(0, 1)
    a0_wait(2)
    a1_start(2, 0)
    for j in (1, 3, 2):
        a1_start(j, 1)
    a1_relay(0)
    for k in range(chunks):
        p_sib(k, False).wait_recv()
    p_near(0, 0)
    p_near(1, 2)
    a1_relay(1)
    a1_relay(3)
    a1_relay(2)
    p_near(0, 1)
    p_near(1, 3)
    for k in (1, 2):
        for j in (0, 1, 3, 2):
            a1_wait(j, k)
    own_gemm()

    def far(*pairs):
        for d, k in pairs:
            p_fwd(d, k, False).wait_recv()
        for d, k in pairs:
            far_gemm(d, k)

    p_near(0, 2)
    p_near(1, 0)
    far((3, 0), (1, 2))
    far((3, 1), (1, 3))
    p_near(0, 3)
    p_near(1, 1)
    far((3, 2), (1, 0))
    p_far(0)
    p_far(2)
    far((3, 3), (1, 1))
    far((2, 0), (2, 2))
    p_far(1)
    p_far(3)
    far((2, 1), (2, 3))

    def col_pass(half, r16):
        strips = 32

        @pl.loop(0, LISTS // (8 * strips))
        def _(i):
            acc = [None] * strips
            for t in range(HT):
                r = jnp.broadcast_to(r16[t : t + 1, :], (8, 128))
                lanes = slice((half * HT + t) * 128, (half * HT + t + 1) * 128)
                for s in range(strips):
                    at = pl.multiple_of(i * (8 * strips) + s * 8, 8)
                    term = K[pl.ds(at, 8), lanes] * r
                    if t == 0 and half == 1:
                        term += csum[pl.ds(at, 8), :]
                    acc[s] = term if acc[s] is None else acc[s] + term
            for s in range(strips):
                csum[pl.ds(pl.multiple_of(i * (8 * strips) + s * 8, 8), 8), :] = acc[s]

    def fold(out):
        parts = []
        for b in range(LT):
            square = csum[b * 128 : (b + 1) * 128, :]
            parts.append(jnp.sum(square.T, axis=0, keepdims=True))
        out[...] = jnp.concatenate(parts, axis=0)

    def col_send(it):
        for k, delta in enumerate(PEERS):
            remote(colbuf.at[it], colrecv.at[it, k], col_s.at[it], col_r.at[it], near(*delta)).start()

    def col_all(it):
        return remote(colrecv.at[it], colrecv.at[it], col_s.at[it], col_r.at[it], near(*PEERS[0]))

    def col_take(it):
        col_all(it).wait_recv()
        return jnp.sum(colrecv[it], axis=0) + colbuf[it]

    def row_pass(half):
        def step(i, acc):
            acc = list(acc)
            for s in range(8):
                at = pl.multiple_of(i * 64 + s * 8, 8)
                scale = cb[pl.ds(at, 8), :]
                for t in range(HT):
                    acc[t] += K[pl.ds(at, 8), (half * HT + t) * 128 : (half * HT + t + 1) * 128] * scale
            return tuple(acc)

        zero = tuple(jnp.zeros((8, 128), F32) for _ in range(HT))
        acc = lax.fori_loop(0, LISTS // 64, step, zero)
        return jnp.concatenate([jnp.sum(a, axis=0, keepdims=True) for a in acc], axis=0)

    row_peers = [up(2, 1 - c), up(2, c)] + [up(d, 1 - c) for d in (1, 3)] + [up(d, c) for d in (1, 3)] + [sibling]

    def row_send(it, half, value):
        rowbuf[it, half] = value
        for k, peer in enumerate(row_peers):
            remote(
                rowbuf.at[it, half], rowrecv.at[it, half, k], row_s.at[it, half], row_r.at[it, half], peer
            ).start()

    def row_all(it, half):
        got = rowrecv.at[it, half]
        return remote(got, got, row_s.at[it, half], row_r.at[it, half], sibling)

    def row_take(it, half):
        row_all(it, half).wait_recv()
        return 1.0 / (jnp.sum(rowrecv[it, half], axis=0) + rowbuf[it, half])

    for it in range(ITERS):
        if it > 0:
            for half in (0, 1):
                col_pass(half, row_take(it - 1, half))
        fold(colbuf.at[it])
        col_send(it)
        c16 = TARGET / col_take(it)
        for b in range(LT):
            cb[b * 128 : (b + 1) * 128, :] = spread(c16[b : b + 1, :])
        for half in (0, 1):
            row_send(it, half, row_pass(half))

    last = {}

    def gemm2(groups, parts=4):
        n = ROWS // parts
        total, mass = None, [None] * len(groups)
        for q in range(parts):
            half = q * 2 // parts
            if half not in last:
                last[half] = row_take(ITERS - 1, half)
            first = q * n // 128 - half * HT
            scale = jnp.concatenate([last[half][t : t + 1, :] for t in range(first, first + n // 128)], axis=1)
            plans = []
            for i, (h, step) in enumerate(groups):
                plan = K[pl.ds(group_at(h, step), GROUP), q * n : (q + 1) * n] * scale
                part = [plan[:, t * 128 : (t + 1) * 128] for t in range(n // 128)]
                while len(part) > 1:
                    part = [part[t] + part[t + 1] for t in range(0, len(part), 2)]
                mass[i] = part[0] if mass[i] is None else mass[i] + part[0]
                plans.append(plan.astype(BF16))
            soft = jnp.dot(jnp.concatenate(plans, axis=0), U[q * n : (q + 1) * n, :], preferred_element_type=F32)
            total = soft if total is None else total + soft
        for i, (h, step) in enumerate(groups):
            csum[pl.ds(group_at(h, step), GROUP), :] = mass[i]
        return [total[i * GROUP : (i + 1) * GROUP, :] for i in range(len(groups))]

    HALF = GROUP // 2

    def cols(w):
        return slice(w * WAVE, (w + 1) * WAVE)

    def rs_copy(h, w, way, k):
        lanes = pl.ds(w * WAVE, WAVE)
        if k == 0:
            src, dst = Sb.at[h, 2, pl.ds(way * HALF, HALF), lanes], Rl.at[h, way, :, lanes]
        else:
            half = 1 - way if k == 1 else way
            src, dst = (b.at[h, way, pl.ds(half * HALF, HALF), lanes] for b in (Sb, Sr))
        return remote(
            src, dst, rs_s.at[h, w, way, k], rs_r.at[h, w, way, k], along(h, 1, 1 if way == 0 else 3)
        )

    def rs_add(h, w, way):
        half = pl.ds(way * HALF, HALF)
        rs_copy(h, w, way, 0).wait_recv()
        Sb[h, way, half, cols(w)] = (Acc[h, way, :, cols(w)] + Rl[h, way, :, cols(w)].astype(F32)).astype(BF16)
        rs_copy(h, w, way, 2).start()

    for h, value in enumerate(gemm2([(0, 2), (1, 2)])):
        Sb[h, 2] = value.astype(BF16)
    for w in (0, 1):
        for h in (0, 1):
            for way in (0, 1):
                rs_copy(h, w, way, 0).start()

    for way in (0, 1):
        values = gemm2([(h, 1 if way == 0 else 3) for h in (0, 1)])
        other = 1 - way
        for h in (0, 1):
            Sb[h, way, pl.ds(other * HALF, HALF), :] = values[h][other * HALF : (other + 1) * HALF, :].astype(BF16)
            Acc[h, way] = values[h][way * HALF : (way + 1) * HALF, :]
        for w in (0, 1):
            for h in (0, 1):
                rs_copy(h, w, way, 1).start()
    for h, value in enumerate(gemm2([(0, 0), (1, 0)])):
        Own[h] = value
    for w in (0, 1):
        for way in (0, 1):
            for h in (0, 1):
                rs_add(h, w, way)
    fold(colbuf.at[ITERS])
    col_send(ITERS)

    def r2_copy(h, w, d):
        lanes = pl.ds(w * WAVE, WAVE)
        return remote(
            Tb.at[h, d - 1, :, lanes], Tr.at[h, d - 1, :, lanes],
            r2_s.at[h, w, d - 1], r2_r.at[h, w, d - 1], along(h, 0, d),
        )

    def sub(h, d):
        return pl.ds(pl.multiple_of((place(h, 0)[0] + d) % 4 * SUB, SUB), SUB)

    for w in (0, 1):
        for h in (0, 1):
            for way in (0, 1):
                for k in (1, 2):
                    rs_copy(h, w, way, k).wait_recv()
            Own[h, :, cols(w)] += Sr[h, 0, :, cols(w)].astype(F32) + Sr[h, 1, :, cols(w)].astype(F32)
            for d in (2, 1, 3):
                Tb[h, d - 1, :, cols(w)] = Own[h, sub(h, d), cols(w)].astype(BF16)
                r2_copy(h, w, d).start()

    colbuf[ITERS + 1] = col_take(ITERS)
    held = []
    for h in (0, 1):
        a, b = place(h, 0)
        wt[...] = spread(colbuf[ITERS + 1, pl.ds(h * 4 + b, 1), :])
        wbuf[pl.ds(h * SUB, SUB), :] = wt[pl.ds(pl.multiple_of(a * SUB, SUB), SUB), :]
        scale = cb[pl.ds(pl.multiple_of(h * HALFLISTS + b * GROUP + a * SUB, SUB), SUB), :]
        held.append(wbuf[pl.ds(h * SUB, SUB), :] * scale)
    mass = jnp.concatenate(held + [jnp.zeros((128 - MINE, 128), F32)], axis=0).T[0:8, :]
    mbuf[dp] = mass
    fin_peers = (
        (dev(zh, 1 - zl, x, y, 1 - c), (1 - zl) * 2 + 1 - c),
        (dev(zh, 1 - zl, x, y, c), (1 - zl) * 2 + c),
        (sibling, zl * 2 + 1 - c),
    )

    def mass_copy(k, sent=True):
        slot = mbuf.at[dp if sent else fin_peers[k][1]]
        return remote(slot, slot, m_s.at[k], m_r.at[k], fin_peers[k][0])

    for k in range(3):
        mass_copy(k).start()

    def fin_copy(k, sent=True):
        to = fin_peers[k][1]
        return remote(Fs.at[to if sent else dp], Fr.at[dp if sent else to], fin_s.at[k], fin_r.at[k], fin_peers[k][0])

    for w in (0, 1):
        for h in (0, 1):
            total = Own[h, sub(h, 0), cols(w)]
            for d in (2, 1, 3):
                r2_copy(h, w, d).wait_recv()
                total += Tr[h, d - 1, :, cols(w)].astype(F32)
            weight = 1.0 / wbuf[pl.ds(h * SUB, SUB), :]
            total *= jnp.concatenate([weight] * (WAVE // 128), axis=1)
            for k in (0, 1):
                Fs[2 * w + k, pl.ds(h * SUB, SUB), :] = total[:, k * WIDTH : (k + 1) * WIDTH].astype(Fs.dtype)
    for k in range(3):
        fin_copy(k).start()

    for k in range(3):
        mass_copy(k, False).wait_recv()
    for k in (0, 1):
        mass_ref[k : k + 1, :] = jnp.concatenate([mbuf[2 * k, 0:1, 0:MINE], mbuf[2 * k + 1, 0:1, 0:MINE]], axis=1)

    mass_out = pltpu.make_async_copy(mass_ref, mass_hbm, out_s.at[1])
    mass_out.start()
    Fr[dp] = Fs[dp]
    for k in (2, 1, 0):
        fin_copy(k, False).wait_recv()
    for k in (0, 1):
        value = jnp.concatenate([Fr[2 * k], Fr[2 * k + 1]], axis=0).astype(F32)
        out_ref[0:128, k * 128 : (k + 1) * 128] = value[:, 0:128].T
        side = jnp.concatenate([value[:, 128:192], jnp.zeros((128, 64), F32)], axis=1)
        out_ref[128:192, k * 128 : (k + 1) * 128] = side.T[0:64, :]

    new_out = pltpu.make_async_copy(out_ref, out_hbm, out_s.at[0])
    new_out.start()

    for h in (0, 1):
        for d in (1, 2, 3):
            a0_copy(h, d).wait_send()
            for w in (0, 1):
                r2_copy(h, w, d).wait_send()
        for way in (0, 1):
            for k in (0, 1, 2):
                for j in range(4):
                    a1_copy(h, j, way, k).wait_send()
                for w in (0, 1):
                    rs_copy(h, w, way, k).wait_send()
    for k in range(chunks):
        for way in (0, 1):
            p_z(k, way).wait_send()
        p_sib(k).wait_send()
        p_relay(k).wait_send()
        for d in (1, 2, 3):
            p_fwd(d, k).wait_send()
    for it in range(ITERS + 1):
        col_all(it).wait_send()
    for it in range(ITERS):
        for half in (0, 1):
            row_all(it, half).wait_send()
    for k in range(3):
        mass_copy(k).wait_send()
        fin_copy(k).wait_send()
    mass_out.wait()
    new_out.wait()


def on_device(passages, centroids):
    lists = centroids.shape[0]
    chunks = OWN // CHUNK
    dma = pltpu.SemaphoreType.DMA
    vm = pltpu.VMEM
    new, mass = pl.pallas_call(
        body,
        out_shape=(
            jax.ShapeDtypeStruct((WIDTH, lists), F32),
            jax.ShapeDtypeStruct((2, 128), F32),
        ),
        in_specs=[pl.BlockSpec(memory_space=pl.ANY)] * 2,
        out_specs=(pl.BlockSpec(memory_space=pl.ANY),) * 2,
        scratch_shapes=[
            vm((WIDTH, lists), F32),
            vm((2, 128), F32),
            vm((OWN, D), BF16),
            vm((MINE, D), BF16),
            vm((ROWS, D), BF16),
            vm((LISTS, D), BF16),
            vm((LISTS, ROWS), F32),
            vm((LISTS, 128), F32),
            vm((LISTS, 128), F32),
            vm((ITERS + 2, LT, 128), F32),
            vm((ITERS + 1, len(PEERS), LT, 128), F32),
            vm((ITERS, 2, HT, 128), F32),
            vm((ITERS, 2, 7, HT, 128), F32),
            vm((2, 3, GROUP, D), BF16),
            vm((2, 2, GROUP, D), BF16),
            vm((2, 2, GROUP // 2, D), BF16),
            vm((2, 2, GROUP // 2, D), F32),
            vm((2, GROUP, D), F32),
            vm((2, 3, SUB, D), BF16),
            vm((2, 3, SUB, D), BF16),
            vm((4, MINE, WIDTH), BF16),
            vm((4, MINE, WIDTH), BF16),
            vm((128, 128), F32),
            vm((MINE, 128), F32),
            vm((4, 8, 128), F32),
            dma((2,)),
            dma((2,)),
            dma((2, 3)), dma((2, 3)),
            dma((2, 4, 2, 3)), dma((2, 4, 2, 3)),
            dma((chunks,)), dma((chunks,)),
            dma((2, chunks)), dma((2, chunks)),
            dma((chunks,)), dma((chunks,)),
            dma((3, chunks)), dma((3, chunks)),
            dma((ITERS + 1,)), dma((ITERS + 1,)),
            dma((ITERS, 2)), dma((ITERS, 2)),
            dma((2, 2, 2, 3)), dma((2, 2, 2, 3)),
            dma((2, 2, 3)), dma((2, 2, 3)),
            dma((3,)), dma((3,)),
            dma((3,)), dma((3,)),
        ],
        compiler_params=pltpu.CompilerParams(
            collective_id=0, has_side_effects=True, vmem_limit_bytes=60 * 1024 * 1024
        ),
        cost_estimate=pl.CostEstimate(
            flops=4 * LISTS * ROWS * D, bytes_accessed=2 * 1024 * 1024, transcendentals=LISTS * ROWS
        ),
        name="sinkhorn",
    )(passages, centroids)
    return new.T, mass.reshape(lists)


def solution(mesh):
    return jax.shard_map(
        on_device,
        mesh=mesh,
        in_specs=(P(("dp", "list"), None), P("list", None)),
        out_specs=(P("list", "dp"), P("list")),
        check_vma=False,
    )
```
